512 devices in a mesh: frame: 32 (over y, x), pix: 16 (over z, core).
Axes of the slice: x: 4, y: 8, z: 8, core: 2. Of those that a mesh axis runs over, the one named last changes fastest.
Arguments:
- query_s: bfloat16 [2, 32, 1024, 576], P(None, 'frame', 'pix'), may hold values from -6 to 6
- key_s: bfloat16 [2, 32, 1024, 576], P(None, 'frame', 'pix'), may hold values from -6 to 6
- value_s: bfloat16 [2, 32, 1024, 576], P(None, 'frame', 'pix'), may hold values from -6 to 6
- query_t: bfloat16 [2, 32, 1024, 576], P(None, 'frame', 'pix'), may hold values from -6 to 6
- key_t: bfloat16 [2, 32, 1024, 576], P(None, 'frame', 'pix'), may hold values from -6 to 6
- value_t: bfloat16 [2, 32, 1024, 576], P(None, 'frame', 'pix'), may hold values from -6 to 6
- grad_out: bfloat16 [2, 32, 1024, 1152], P(None, 'frame', 'pix'), may hold values from -6 to 6
- proj_s: bfloat16 [576, 1152], replicated, may hold values from -0.25 to 0.25
- proj_t: bfloat16 [576, 1152], replicated, may hold values from -0.25 to 0.25
Outputs:
- grad_query_s: bfloat16 [2, 32, 1024, 576], P(None, 'frame', 'pix')
- grad_key_s: bfloat16 [2, 32, 1024, 576], P(None, 'frame', 'pix')
- grad_value_s: bfloat16 [2, 32, 1024, 576], P(None, 'frame', 'pix')
- grad_query_t: bfloat16 [2, 32, 1024, 576], P(None, 'frame', 'pix')
- grad_key_t: bfloat16 [2, 32, 1024, 576], P(None, 'frame', 'pix')
- grad_value_t: bfloat16 [2, 32, 1024, 576], P(None, 'frame', 'pix')
- grad_proj_s: float32 [576, 1152], P('frame', 'pix')
- grad_proj_t: float32 [576, 1152], P('frame', 'pix')
The draws below stay inside these ranges and needn't reach their ends.
All inputs are finite; a program needn't handle non-finite values.
Results may differ from the reference program's by a relative error of at most 0.034.
Values may be sent and summed in bfloat16 or wider, within the bound.
No kernel may reach another device: no remote copies, remote signals or barrier semaphores. Data moves between devices by JAX's collectives and lax.ppermute only.
A program may use at most 128 MiB of HBM per device.

```python
import jax
import jax.numpy as jnp
from jax import lax

D = 1152
HSIZE = 72
HEADS = 8
CLIPS = 2
PIX_DEV = 64
HD = 576
FRAMES = 32
TOKF = 1024
N_PIX = 16


slot_count = 4


peak_level = 6.0


def signed_levels(key, extent):
    return (2 * jax.random.randint(key, extent, 0, 2) - 1).astype(jnp.float32)


def runner_up(signs, power):
    markers = (jnp.arange(HD) % HSIZE == 0).astype(jnp.float32)
    shortfall = 2.0 * HSIZE ** 0.5 / power
    return signs * (peak_level - shortfall[..., None] * markers)


def spatial_plan(key):
    key = jax.random.fold_in(key, 101)
    key_places, key_signs, key_power = jax.random.split(key, 3)
    subkeys = jax.random.split(key_places, CLIPS * FRAMES)
    places = jax.vmap(lambda single: jax.random.permutation(single, TOKF)[:3 * slot_count])(subkeys)
    places = places.reshape(CLIPS, FRAMES, 3 * slot_count)
    signs = signed_levels(key_signs, (CLIPS, FRAMES, slot_count, HD))
    power = jax.random.randint(key_power, (CLIPS, FRAMES, slot_count), 4, 7).astype(jnp.float32)
    return (places, signs, power)


def temporal_plan(key):
    key = jax.random.fold_in(key, 202)
    key_places, key_frames, key_signs, key_power = jax.random.split(key, 4)
    slot_total = min(slot_count * FRAMES, TOKF)
    places = jax.vmap(lambda single: jax.random.permutation(single, TOKF)[:slot_total])(jax.random.split(key_places, CLIPS))
    picks = jax.vmap(lambda single: jax.random.permutation(single, FRAMES)[:3])(jax.random.split(key_frames, CLIPS * slot_total))
    picks = picks.reshape(CLIPS, slot_total, 3)
    signs = signed_levels(key_signs, (CLIPS, slot_total, HD))
    power = jax.random.randint(key_power, (CLIPS, slot_total), 4, 7).astype(jnp.float32)
    return (places, picks, signs, power)


def draw_query_s(key, part):
    places, signs, power = spatial_plan(key)
    key = jax.random.fold_in(key, 1)
    full_shape = (CLIPS, FRAMES, TOKF, HD)
    sample = jnp.clip(jax.random.normal(key, full_shape), -6.0, 6.0)
    clip_index = jnp.arange(CLIPS)[:, None, None]
    frame_index = jnp.arange(FRAMES)[None, :, None]
    sample = sample.at[clip_index, frame_index, places[..., :slot_count]].set(power[..., None] * signs)
    return sample.astype(jnp.bfloat16)


def draw_key_s(key, part):
    places, signs, power = spatial_plan(key)
    key = jax.random.fold_in(key, 2)
    full_shape = (CLIPS, FRAMES, TOKF, HD)
    sample = jnp.clip(jax.random.normal(key, full_shape), -6.0, 6.0)
    clip_index = jnp.arange(CLIPS)[:, None, None]
    frame_index = jnp.arange(FRAMES)[None, :, None]
    sample = sample.at[clip_index, frame_index, places[..., slot_count:2 * slot_count]].set(peak_level * signs)
    sample = sample.at[clip_index, frame_index, places[..., 2 * slot_count:]].set(runner_up(signs, power))
    return sample.astype(jnp.bfloat16)


def draw_query_t(key, part):
    places, picks, signs, power = temporal_plan(key)
    key = jax.random.fold_in(key, 3)
    full_shape = (CLIPS, FRAMES, TOKF, HD)
    sample = jnp.clip(jax.random.normal(key, full_shape), -6.0, 6.0)
    clip_index = jnp.arange(CLIPS)[:, None]
    sample = sample.at[clip_index, picks[..., 0], places].set(power[..., None] * signs)
    return sample.astype(jnp.bfloat16)


def draw_key_t(key, part):
    places, picks, signs, power = temporal_plan(key)
    key = jax.random.fold_in(key, 4)
    full_shape = (CLIPS, FRAMES, TOKF, HD)
    sample = jnp.clip(jax.random.normal(key, full_shape), -6.0, 6.0)
    clip_index = jnp.arange(CLIPS)[:, None]
    sample = sample.at[clip_index, picks[..., 1], places].set(peak_level * signs)
    sample = sample.at[clip_index, picks[..., 2], places].set(runner_up(signs, power))
    return sample.astype(jnp.bfloat16)


def block_levels(own_key, shape, cuts, low, largest):
    factor_of, own = 1.0, jax.random.fold_in(own_key, 6)
    for position, parts in cuts:
        steps = jnp.exp(jax.random.uniform(jax.random.fold_in(own, position), (parts,), jnp.float32, low / len(cuts), largest / len(cuts)))
        factor_of = factor_of * jnp.repeat(steps, shape[position] // parts).reshape([-1 if axis == position else 1 for axis in range(len(shape))])
    return factor_of


def centred(rng, shape, deviation, reach, cuts=(), held_as=jnp.bfloat16):
    array = deviation * jax.random.normal(rng, shape, jnp.float32)
    if cuts:
        array = array * block_levels(rng, shape, cuts, -0.22, 0.18)
    return jnp.clip(array, -reach, reach).astype(held_as)


def setup_inputs(seed: int = 0) -> dict:
    streams_of = jax.random.split(jax.random.key(seed), 10)
    query_s = draw_query_s(jax.random.fold_in(streams_of[9], 71), 0)
    key_s = draw_key_s(jax.random.fold_in(streams_of[9], 71), 0)
    value_s = centred(streams_of[2], (CLIPS, FRAMES, TOKF, HD), 1.0, 6.0, ((1, 32), (2, 16)))
    query_t = draw_query_t(jax.random.fold_in(streams_of[9], 71), 0)
    key_t = draw_key_t(jax.random.fold_in(streams_of[9], 71), 0)
    value_t = centred(streams_of[5], (CLIPS, FRAMES, TOKF, HD), 1.0, 6.0, ((1, 32), (2, 16)))
    grad_out = centred(streams_of[6], (CLIPS, FRAMES, TOKF, D), 1.0, 6.0, ((1, 32), (2, 16)))
    proj_s = centred(streams_of[7], (HD, D), HD ** -0.5, 0.25)
    proj_t = centred(streams_of[8], (HD, D), HD ** -0.5, 0.25)
    return dict(query_s=query_s, key_s=key_s, value_s=value_s, query_t=query_t, key_t=key_t, value_t=value_t, grad_out=grad_out, proj_s=proj_s, proj_t=proj_t)


def rounded(value):
    return lax.optimization_barrier(value.astype(jnp.bfloat16)).astype(jnp.float32)

def attend(queries, key_rows, value_rows):
    factor = HSIZE ** (-0.5)
    scores = jnp.einsum('bqhe,bkhe->bhqk', queries.astype(jnp.float32), key_rows.astype(jnp.float32)) * factor
    highest = scores.max(-1, keepdims=True)
    exp_scores = jnp.exp(scores - highest)
    totals = exp_scores.sum(-1)
    mixed = jnp.einsum('bhqk,bkhe->bqhe', rounded(exp_scores), value_rows.astype(jnp.float32))
    mixed = mixed / totals.transpose(0, 2, 1)[..., None]
    return (mixed.astype(jnp.bfloat16), highest[..., 0] + jnp.log(totals))

def attend_back(queries, key_rows, value_rows, outputs, log_totals, grad_outputs):
    factor = HSIZE ** (-0.5)
    query_f = queries.astype(jnp.float32)
    key_f = key_rows.astype(jnp.float32)
    grad_f = grad_outputs.astype(jnp.float32)
    scores = jnp.einsum('bqhe,bkhe->bhqk', query_f, key_f) * factor
    weights = jnp.exp(scores - log_totals[..., None])
    grad_values = jnp.einsum('bhqk,bqhe->bkhe', rounded(weights), grad_f).astype(jnp.bfloat16)
    dprob = jnp.einsum('bqhe,bkhe->bhqk', grad_f, value_rows.astype(jnp.float32))
    delta = lax.optimization_barrier(jnp.sum(grad_f * outputs.astype(jnp.float32), -1)).transpose(0, 2, 1)
    dscore = rounded(weights * (dprob - delta[..., None]))
    grad_queries = (factor * jnp.einsum('bhqk,bkhe->bqhe', dscore, key_f)).astype(jnp.bfloat16)
    grad_keys = (factor * jnp.einsum('bhqk,bqhe->bkhe', dscore, query_f)).astype(jnp.bfloat16)
    return (grad_queries, grad_keys, grad_values)

def both_ways(queries, key_rows, value_rows, grad_outputs):
    outputs, log_totals = attend(queries, key_rows, value_rows)
    grads = attend_back(queries, key_rows, value_rows, outputs, log_totals, grad_outputs)
    return (outputs, grads[0], grads[1], grads[2])

def spatial_item(stacked):
    pieces = [piece.reshape(1, TOKF, HEADS, HSIZE) for piece in stacked]
    result = both_ways(pieces[0], pieces[1], pieces[2], pieces[3])
    return tuple((piece.reshape(TOKF, HD) for piece in result))

def temporal_item(stacked):
    pieces = [piece.reshape(TOKF, FRAMES, HEADS, HSIZE) for piece in stacked]
    result = both_ways(pieces[0], pieces[1], pieces[2], pieces[3])
    return tuple((piece.reshape(TOKF, FRAMES, HD) for piece in result))

def frame_sum(pair):
    outputs, grads = pair
    partial_sums = jnp.einsum('cpte,cptd->ped', outputs.astype(jnp.float32), grads.astype(jnp.float32))
    partial_sums = rounded(partial_sums)
    return lax.optimization_barrier(jnp.sum(partial_sums, 0)).astype(jnp.bfloat16)

def projection_grad(outputs, grad_out):
    shaped_out = outputs.reshape(CLIPS, FRAMES, N_PIX, PIX_DEV, HD).transpose(1, 0, 2, 3, 4)
    shaped_grad = grad_out.reshape(CLIPS, FRAMES, N_PIX, PIX_DEV, D).transpose(1, 0, 2, 3, 4)
    per_frame = lax.map(frame_sum, (shaped_out, shaped_grad))
    return lax.optimization_barrier(jnp.sum(per_frame.astype(jnp.float32), 0))

def reference(query_s, key_s, value_s, query_t, key_t, value_t, grad_out, proj_s, proj_t):
    flat_grad = grad_out.reshape(-1, D)
    grad_o_s = jnp.dot(flat_grad, proj_s.T, preferred_element_type=jnp.float32).astype(jnp.bfloat16)
    grad_o_t = jnp.dot(flat_grad, proj_t.T, preferred_element_type=jnp.float32).astype(jnp.bfloat16)
    grad_o_s = grad_o_s.reshape(CLIPS, FRAMES, TOKF, HD)
    grad_o_t = grad_o_t.reshape(CLIPS, FRAMES, TOKF, HD)
    spatial_in = tuple((piece.reshape(CLIPS * FRAMES, TOKF, HD) for piece in (query_s, key_s, value_s, grad_o_s)))
    spatial_res = lax.map(spatial_item, spatial_in)
    spatial_res = [piece.reshape(CLIPS, FRAMES, TOKF, HD) for piece in spatial_res]
    temporal_in = tuple((piece.transpose(0, 2, 1, 3) for piece in (query_t, key_t, value_t, grad_o_t)))
    temporal_res = lax.map(temporal_item, temporal_in)
    temporal_res = [piece.transpose(0, 2, 1, 3) for piece in temporal_res]
    grad_proj_s = projection_grad(spatial_res[0], grad_out)
    grad_proj_t = projection_grad(temporal_res[0], grad_out)
    return (spatial_res[1], spatial_res[2], spatial_res[3], temporal_res[1], temporal_res[2], temporal_res[3], grad_proj_s, grad_proj_t)
```

```python
import jax
import jax.numpy as jnp
from jax import lax
from jax.experimental import pallas as pl
from jax.experimental.pallas import tpu as pltpu
from jax.sharding import PartitionSpec as P

HSIZE = 72
HEADS = 8
HD = 576
WIDE = 640
D = 1152
HALF = 576
FACTOR = HSIZE ** (-0.5)
BF = jnp.bfloat16
F32 = jnp.float32


def dot(a, b):
    return lax.dot_general(a, b, (((1,), (0,)), ((), ())), preferred_element_type=F32)


def dot_nt(a, b):
    return lax.dot_general(a, b, (((1,), (1,)), ((), ())), preferred_element_type=F32)


def iota(shape, dim):
    return lax.broadcasted_iota(jnp.int32, shape, dim)


def choose(cond):
    return jnp.where(cond, 1.0, 0.0).astype(BF)


def window(h):
    start = (HSIZE * h) // 128 * 128
    return start, min(256, HD - start), HSIZE * h - start


def core_columns(core):
    col = iota((D, HALF), 1)
    z = col // HSIZE
    return choose(iota((D, HALF), 0) == col + HSIZE * z + HSIZE * core)


def whole(shape, dtype):
    return jax.ShapeDtypeStruct(shape, dtype)


def call(kernel, n_in, out_shape, flops, scalars=0, scratch=()):
    many = isinstance(out_shape, (tuple, list))
    vmem = pl.BlockSpec(memory_space=pltpu.VMEM)
    smem = pl.BlockSpec(memory_space=pltpu.SMEM)
    return pl.pallas_call(
        kernel,
        out_shape=out_shape,
        in_specs=[smem] * scalars + [vmem] * n_in,
        out_specs=[vmem] * len(out_shape) if many else vmem,
        scratch_shapes=list(scratch),
        compiler_params=pltpu.CompilerParams(vmem_limit_bytes=32 * 1024 * 1024),
        cost_estimate=pl.CostEstimate(flops=flops, bytes_accessed=1 << 20, transcendentals=0),
    )


def pack_kernel(q_ref, k_ref, v_ref, out_ref):
    rows = q_ref.shape[0] // 2
    for h in range(HEADS):
        start, width, offset = window(h)
        total = None
        for a, ref in enumerate((q_ref, k_ref, v_ref)):
            i, j = iota((width, 256), 0), iota((width, 256), 1) - HSIZE * a
            sel = choose((i - offset == j) & (j >= 0) & (j < HSIZE))
            part = dot(ref[:, start : start + width], sel)
            total = part if total is None else total + part
        total = total.astype(BF)[:, : 3 * HSIZE]
        out_ref[2 * h] = total[:rows]
        out_ref[2 * h + 1] = total[rows:]


def unpack_kernel(x_ref, *out_refs):
    rows = x_ref.shape[1]
    for a, ref in enumerate(out_refs):
        for start in range(0, HD, 128):
            width = min(128, HD - start)
            total = None
            for h in range(HEADS):
                low = HSIZE * h - start
                if low >= width or low + HSIZE <= 0:
                    continue
                pair = jnp.concatenate([x_ref[2 * h], x_ref[2 * h + 1]], 0)
                i, j = iota((3 * HSIZE, width), 0) - HSIZE * a, iota((3 * HSIZE, width), 1)
                sel = choose((i + low == j) & (i >= 0) & (i < HSIZE))
                part = dot(pair, sel)
                total = part if total is None else total + part
            ref[:, start : start + width] = total.astype(BF)


def spatial_kernel(core_ref, x_ref, g_ref, proj_ref, out_ref, keep_ref, send_ref, dkt_ref, dvt_ref):
    core = core_ref[0]
    rows = x_ref.shape[0]
    pairs = rows // 128
    step = 256

    def swapped(value):
        parts = value.reshape(pairs, 2, 64, value.shape[1])
        other = jnp.concatenate([parts[:, 1:], parts[:, :1]], 1)
        return jnp.where(core == 0, parts, other).reshape(value.shape)

    i, j = iota((3 * HSIZE, 384), 0), iota((3 * HSIZE, 384), 1)
    sel = choose((i == HSIZE * (j // 128) + j % 128) & (j % 128 < HSIZE))
    split = dot(x_ref[...], sel)
    queries = split[:, :128]
    queries_bf = queries.astype(BF)
    keys = split[:, 128:256].astype(BF)
    values = split[:, 256:].astype(BF)
    grads = swapped(dot_nt(g_ref[...], proj_ref[...])).astype(BF).astype(F32)
    grads_bf = grads.astype(BF)
    outs = []
    dqs = []
    for b in range(rows // step):
        block = slice(b * step, (b + 1) * step)
        q, do = queries[block], grads[block]
        q_bf, do_bf = queries_bf[block], grads_bf[block]
        scores = dot_nt(q_bf, keys) * FACTOR
        top = scores.max(-1, keepdims=True)
        e = jnp.exp(scores - top)
        inverse = 1.0 / e.sum(-1, keepdims=True)
        out = (dot(e.astype(BF), values) * inverse).astype(BF).astype(F32)
        outs.append(out)
        weights = e * inverse
        delta = (do * out).sum(-1, keepdims=True)
        dprob = dot_nt(do_bf, values)
        dscore = (weights * (dprob - delta)).astype(BF)
        dqs.append(dot(dscore, keys) * FACTOR)
        dkt = dot(q.T.astype(BF), dscore)
        dvt = dot(do.T.astype(BF), weights.astype(BF))
        if b == 0:
            dkt_ref[...] = dkt
            dvt_ref[...] = dvt
        else:
            dkt_ref[...] += dkt
            dvt_ref[...] += dvt
    grads_all = jnp.concatenate(
        [jnp.concatenate(dqs, 0), dkt_ref[...].T * FACTOR, dvt_ref[...].T], 1
    ).astype(BF)
    out_ref[...] = dot_nt(grads_all, sel).astype(BF)
    out_all = swapped(jnp.concatenate(outs, 0))
    part = dot(out_all.T.astype(BF), g_ref[...]).astype(BF)
    keep_ref[...] = dot(part, core_columns(core)).astype(BF)[:HSIZE]
    send_ref[...] = dot(part, core_columns(1 - core)).astype(BF)[:HSIZE]


def temporal_kernel(core_ref, x_ref, proj_ref, out_ref, keep_ref, send_ref):
    core = core_ref[0]
    rows = x_ref.shape[0]
    group = 4
    q = x_ref[:, :HD]
    k = x_ref[:, WIDE : WIDE + HD]
    v = x_ref[:, 2 * WIDE : 2 * WIDE + HD]
    g = x_ref[:, 3 * WIDE :]
    do = dot_nt(g, proj_ref[...]).astype(BF)
    same = iota((rows, rows), 0) % group == iota((rows, rows), 1) % group
    head = iota((1, HD), 1) // HSIZE
    masks = [choose(head == h) for h in range(HEADS)]
    weights = []
    out = None
    for h in range(HEADS):
        scores = jnp.where(same, dot_nt(q * masks[h], k) * FACTOR, -1e30)
        e = jnp.where(same, jnp.exp(scores - scores.max(-1, keepdims=True)), 0.0)
        inverse = 1.0 / e.sum(-1, keepdims=True)
        part = dot(e.astype(BF), v * masks[h]) * inverse
        out = part if out is None else out + part
        weights.append(e * inverse)
    out = out.astype(BF)
    product = do.astype(F32) * out.astype(F32)
    dq = dk = dv = None
    for h in range(HEADS):
        dom = do * masks[h]
        delta = (product * masks[h].astype(F32)).sum(-1, keepdims=True)
        dscore = weights[h] * (dot_nt(dom, v) - delta)
        terms = (
            dot(dscore.astype(BF), k * masks[h]),
            dot(dscore.T.astype(BF), q * masks[h]),
            dot(weights[h].T.astype(BF), dom),
        )
        dq, dk, dv = terms if dq is None else (dq + terms[0], dk + terms[1], dv + terms[2])
    out_ref[:, :HD] = (dq * FACTOR).astype(BF)
    out_ref[:, WIDE : WIDE + HD] = (dk * FACTOR).astype(BF)
    out_ref[:, 2 * WIDE : 2 * WIDE + HD] = dv.astype(BF)
    i, j = iota((HD, HD), 0), iota((HD, HD), 1)
    order = choose(j == 18 * (i % 64 // 2) + 2 * (i // 64) + i % 2)
    out_t = dot_nt(order, out).astype(BF)
    for ref, half in ((keep_ref, core), (send_ref, 1 - core)):
        part = dot(out_t, dot(g, core_columns(half)).astype(BF)).astype(BF)
        ref[...] = jnp.zeros(ref.shape, BF)
        for b in range(9):
            ref[:, WIDE * b : WIDE * b + HALF] = part[64 * b : 64 * b + 64]


def on_device(query_s, key_s, value_s, query_t, key_t, value_t, grad_out, proj_s, proj_t):
    frames = lax.axis_size("frame")
    n_pix = lax.axis_size("pix")
    n_z = n_pix // 2
    pix = lax.axis_index("pix")
    core, z = pix % 2, pix // 2
    core_arg = core.reshape(1).astype(jnp.int32)
    core_swap = [(p, p ^ 1) for p in range(n_pix)]
    same_core = [[2 * i + c for i in range(n_z)] for c in range(2)]

    with jax.named_scope("spatial_grad_gather"):
        grad = grad_out[:, 0]
        own = lax.dynamic_index_in_dim(grad, core, 0, keepdims=False)
        other = lax.dynamic_index_in_dim(grad, 1 - core, 0, keepdims=False)
        other = lax.ppermute(other, "pix", core_swap)
        gathered = lax.all_gather(
            jnp.concatenate([own, other], 0), "pix", axis=0, axis_index_groups=same_core, tiled=True
        )

    with jax.named_scope("temporal_in"):
        spread = [jnp.pad(a[:, 0], ((0, 0), (0, 0), (0, WIDE - HD))) for a in (query_t, key_t, value_t)]
        rows = jnp.concatenate(spread + [grad], -1).reshape(4, frames, 3 * WIDE + D)
        moved_t = lax.all_to_all(rows.transpose(1, 0, 2), "frame", 0, 0, tiled=True)
        moved_t = moved_t.reshape(4 * frames, 3 * WIDE + D)

    with jax.named_scope("spatial_in"):
        flat = [a.reshape(128, HD) for a in (query_s, key_s, value_s)]
        packed = call(pack_kernel, 3, whole((n_pix, 64, 3 * HSIZE), BF), 1 << 26)(*flat)
        moved_s = lax.all_to_all(packed, "pix", 0, 0, tiled=True)

    with jax.named_scope("temporal_attention"):
        grads_t, keep_t, send_t = call(
            temporal_kernel,
            2,
            (
                whole((4 * frames, 3 * WIDE), BF),
                whole((64, 9 * WIDE), BF),
                whole((64, 9 * WIDE), BF),
            ),
            1 << 30,
            scalars=1,
        )(core_arg, moved_t, proj_t)
        total_t = keep_t.astype(F32) + lax.ppermute(send_t, "pix", core_swap).astype(F32)
        total_t = total_t.astype(BF).reshape(frames, 2, 9 * WIDE)

    with jax.named_scope("spatial_attention"):
        proj_h = lax.dynamic_slice_in_dim(proj_s, HSIZE * z, HSIZE, 0)
        proj_h = jnp.pad(proj_h, ((0, 128 - HSIZE), (0, 0)))
        grads_s, keep_s, send_s = call(
            spatial_kernel,
            3,
            (
                whole((n_pix * 64, 3 * HSIZE), BF),
                whole((HSIZE, HALF), BF),
                whole((HSIZE, HALF), BF),
            ),
            1 << 32,
            scalars=1,
            scratch=[pltpu.VMEM((128, n_pix * 64), F32)] * 2,
        )(core_arg, moved_s.reshape(n_pix * 64, 3 * HSIZE), gathered, proj_h)
        total_s = keep_s.astype(F32) + lax.ppermute(send_s, "pix", core_swap).astype(F32)

    with jax.named_scope("temporal_out"):
        home_t = lax.all_to_all(grads_t.reshape(frames, 4, 3 * WIDE), "frame", 0, 0, tiled=True)
        home_t = home_t.transpose(1, 0, 2).reshape(2, 1, 64, 3 * WIDE)
        outs_t = [home_t[..., WIDE * a : WIDE * a + HD] for a in range(3)]

    with jax.named_scope("temporal_projection"):
        parts_t = lax.all_to_all(total_t, "frame", 0, 0, tiled=True)
        sums_t = parts_t.astype(F32).sum(0).astype(BF).reshape(2, 9, WIDE)[..., :HALF]
        sums_t = sums_t.reshape(2, 9, n_z, HSIZE).transpose(2, 1, 0, 3).reshape(n_z, 18, HSIZE)
        last_t = lax.all_to_all(sums_t, "pix", 0, 0, axis_index_groups=same_core, tiled=True)
        proj_t_grad = last_t.astype(F32).sum(0)

    with jax.named_scope("spatial_projection"):
        chunks = total_s.astype(BF).reshape(4, 18, 8, HSIZE).transpose(2, 0, 1, 3)
        parts_s = lax.all_to_all(chunks.reshape(frames, 18, HSIZE), "frame", 0, 0, tiled=True)
        sums_s = parts_s.astype(F32).sum(0)
        perm = []
        for y in range(8):
            for x in range(4):
                for zz in range(n_z):
                    for c in range(2):
                        source = (y * 4 + x) * n_pix + 2 * zz + c
                        perm.append((source, (zz * 4 + x) * n_pix + 2 * y + c))
        proj_s_grad = lax.ppermute(sums_s, ("frame", "pix"), perm)

    with jax.named_scope("spatial_out"):
        home_s = lax.all_to_all(grads_s.reshape(n_pix, 64, 3 * HSIZE), "pix", 0, 0, tiled=True)
        outs_s = call(unpack_kernel, 1, (whole((128, HD), BF),) * 3, 1 << 26)(home_s)
        outs_s = [a.reshape(2, 1, 64, HD) for a in outs_s]

    return (*outs_s, *outs_t, proj_s_grad, proj_t_grad)


def solution(mesh):
    rows = P(None, "frame", "pix", None)
    out_specs = (rows,) * 6 + (P("frame", "pix"),) * 2
    return jax.shard_map(
        on_device,
        mesh=mesh,
        in_specs=(rows,) * 7 + (P(), P()),
        out_specs=out_specs,
        check_vma=False,
    )
```

```python
import jax
import jax.numpy as jnp
from jax import lax
from jax.experimental import pallas as pl
from jax.experimental.pallas import tpu as pltpu
from jax.sharding import PartitionSpec as P

HSIZE = 72
HEADS = 8
HD = 576
D = 1152
HALF = 576
GRADS = 6 * HD
SUMS_T = 9 * HALF
SUMS_S = 9 * 2 * HSIZE
FACTOR = HSIZE ** (-0.5)
BF = jnp.bfloat16
F32 = jnp.float32


def dot(a, b):
    return lax.dot_general(a, b, (((1,), (0,)), ((), ())), preferred_element_type=F32)


def dot_nt(a, b):
    return lax.dot_general(a, b, (((1,), (1,)), ((), ())), preferred_element_type=F32)


def iota(shape, dim):
    return lax.broadcasted_iota(jnp.int32, shape, dim)


def choose(cond):
    return jnp.where(cond, 1.0, 0.0).astype(BF)


def window(h):
    start = (HSIZE * h) // 128 * 128
    return start, min(256, HD - start), HSIZE * h - start


def core_columns(core):
    col = iota((D, HALF), 1)
    z = col // HSIZE
    return choose(iota((D, HALF), 0) == col + HSIZE * z + HSIZE * core)


def whole(shape, dtype):
    return jax.ShapeDtypeStruct(shape, dtype)


def call(kernel, n_in, out_shape, flops, scalars=0, scratch=()):
    many = isinstance(out_shape, (tuple, list))
    vmem = pl.BlockSpec(memory_space=pltpu.VMEM)
    smem = pl.BlockSpec(memory_space=pltpu.SMEM)
    return pl.pallas_call(
        kernel,
        out_shape=out_shape,
        in_specs=[smem] * scalars + [vmem] * n_in,
        out_specs=[vmem] * len(out_shape) if many else vmem,
        scratch_shapes=list(scratch),
        compiler_params=pltpu.CompilerParams(vmem_limit_bytes=32 * 1024 * 1024),
        cost_estimate=pl.CostEstimate(flops=flops, bytes_accessed=1, transcendentals=0),
    )


def pack_kernel(q_ref, k_ref, v_ref, out_ref):
    rows = q_ref.shape[0] // 2
    for h in range(HEADS):
        start, width, offset = window(h)
        total = None
        for a, ref in enumerate((q_ref, k_ref, v_ref)):
            i, j = iota((width, 256), 0), iota((width, 256), 1) - HSIZE * a
            sel = choose((i - offset == j) & (j >= 0) & (j < HSIZE))
            part = dot(ref[:, start : start + width], sel)
            total = part if total is None else total + part
        total = total.astype(BF)[:, : 3 * HSIZE]
        out_ref[2 * h] = total[:rows]
        out_ref[2 * h + 1] = total[rows:]


def unpack_kernel(x_ref, *out_refs):
    rows = x_ref.shape[1]
    for a, ref in enumerate(out_refs):
        for start in range(0, HD, 128):
            width = min(128, HD - start)
            total = None
            for h in range(HEADS):
                low = HSIZE * h - start
                if low >= width or low + HSIZE <= 0:
                    continue
                pair = jnp.concatenate([x_ref[2 * h], x_ref[2 * h + 1]], 0)[:, : 3 * HSIZE]
                i, j = iota((3 * HSIZE, width), 0) - HSIZE * a, iota((3 * HSIZE, width), 1)
                sel = choose((i + low == j) & (i >= 0) & (i < HSIZE))
                part = dot(pair, sel)
                total = part if total is None else total + part
            ref[:, start : start + width] = total.astype(BF)


def spatial_kernel(core_ref, x_ref, g_ref, proj_ref, out_ref, part_ref, dkt_ref, dvt_ref, chunk_ref):
    core = core_ref[0]
    rows = x_ref.shape[0]
    pairs = rows // 128
    step = 256

    def swapped(value):
        parts = value.reshape(pairs, 2, 64, value.shape[1])
        other = jnp.concatenate([parts[:, 1:], parts[:, :1]], 1)
        return jnp.where(core == 0, parts, other).reshape(value.shape)

    i, j = iota((3 * HSIZE, 384), 0), iota((3 * HSIZE, 384), 1)
    sel = choose((i == HSIZE * (j // 128) + j % 128) & (j % 128 < HSIZE))
    split = dot(x_ref[...], sel)
    queries = split[:, :128]
    queries_bf = queries.astype(BF)
    keys = split[:, 128:256].astype(BF)
    values = split[:, 256:].astype(BF)
    grads = swapped(dot_nt(g_ref[...], proj_ref[...])).astype(BF).astype(F32)
    grads_bf = grads.astype(BF)
    outs = []
    dqs = []
    for b in range(rows // step):
        block = slice(b * step, (b + 1) * step)
        q, do = queries[block], grads[block]
        q_bf, do_bf = queries_bf[block], grads_bf[block]
        scores = dot_nt(q_bf, keys) * FACTOR
        top = scores.max(-1, keepdims=True)
        e = jnp.exp(scores - top)
        inverse = 1.0 / e.sum(-1, keepdims=True)
        out = (dot(e.astype(BF), values) * inverse).astype(BF).astype(F32)
        outs.append(out)
        weights = e * inverse
        delta = (do * out).sum(-1, keepdims=True)
        dprob = dot_nt(do_bf, values)
        dscore = (weights * (dprob - delta)).astype(BF)
        dqs.append(dot(dscore, keys) * FACTOR)
        dkt = dot(q.T.astype(BF), dscore)
        dvt = dot(do.T.astype(BF), weights.astype(BF))
        if b == 0:
            dkt_ref[...] = dkt
            dvt_ref[...] = dvt
        else:
            dkt_ref[...] += dkt
            dvt_ref[...] += dvt
    grads_all = jnp.concatenate(
        [jnp.concatenate(dqs, 0), dkt_ref[...].T * FACTOR, dvt_ref[...].T], 1
    ).astype(BF)
    out_ref[...] = dot_nt(grads_all, sel).astype(BF)
    out_all = swapped(jnp.concatenate(outs, 0))
    part = dot(out_all.T.astype(BF), g_ref[...]).astype(BF)
    i, j = iota((HSIZE, 128), 0), iota((HSIZE, 128), 1)
    part = dot(choose(j == 18 * (i % 8 // 2) + 2 * (i // 8) + i % 2), part)
    wide = 2 * HSIZE
    for y in range(8):
        columns = part[:, wide * y : wide * (y + 1)]
        for b in range(9):
            chunk_ref[8 * y : 8 * (y + 1), wide * b : wide * (b + 1)] = columns[8 * b : 8 * (b + 1)]
    part_ref[...] = chunk_ref[...].astype(BF)


def pack_time_kernel(q_ref, k_ref, v_ref, g_ref, out_ref):
    rows, frames = q_ref.shape[0], out_ref.shape[0]
    group = rows // frames
    i, j = iota((rows, rows), 0), iota((rows, rows), 1)
    order = choose(j == frames * (i % group) + i // group)
    moved = [dot(order, ref[...]).astype(BF) for ref in (q_ref, k_ref, v_ref, g_ref)]
    moved = jnp.concatenate(moved, 1)
    for f in range(frames):
        out_ref[f] = moved[group * f : group * (f + 1)]


def merge_kernel(grads_ref, keep_ref, got_ref, part_ref, out_ref):
    total = (keep_ref[...].astype(F32) + got_ref[...].astype(F32)).astype(BF)
    for f in range(out_ref.shape[0]):
        rows = slice(2 * f, 2 * f + 2)
        out_ref[f, :, :GRADS] = grads_ref[rows]
        out_ref[f, :, GRADS : GRADS + SUMS_T] = total[rows]
        out_ref[f, :, GRADS + SUMS_T :] = part_ref[rows]


def temporal_kernel(core_ref, x_ref, proj_ref, out_ref, keep_ref, send_ref):
    core = core_ref[0]
    rows = x_ref.shape[0]
    group = 4
    q, k, v = [x_ref[:, HD * a : HD * (a + 1)] for a in range(3)]
    g = x_ref[:, 3 * HD :]
    do = dot_nt(g, proj_ref[...]).astype(BF)
    same = iota((rows, rows), 0) % group == iota((rows, rows), 1) % group
    head = iota((1, HD), 1) // HSIZE
    masks = [choose(head == h) for h in range(HEADS)]
    weights = []
    out = None
    for h in range(HEADS):
        scores = jnp.where(same, dot_nt(q * masks[h], k) * FACTOR, -1e30)
        e = jnp.where(same, jnp.exp(scores - scores.max(-1, keepdims=True)), 0.0)
        inverse = 1.0 / e.sum(-1, keepdims=True)
        part = dot(e.astype(BF), v * masks[h]) * inverse
        out = part if out is None else out + part
        weights.append(e * inverse)
    out = out.astype(BF)
    product = do.astype(F32) * out.astype(F32)
    dq = dk = dv = None
    for h in range(HEADS):
        dom = do * masks[h]
        delta = (product * masks[h].astype(F32)).sum(-1, keepdims=True)
        dscore = weights[h] * (dot_nt(dom, v) - delta)
        terms = (
            dot(dscore.astype(BF), k * masks[h]),
            dot(dscore.T.astype(BF), q * masks[h]),
            dot(weights[h].T.astype(BF), dom),
        )
        dq, dk, dv = terms if dq is None else (dq + terms[0], dk + terms[1], dv + terms[2])
    i, j = iota((rows, rows), 0), iota((rows, rows), 1)
    half_rows = rows // 2
    order = choose(j == group * (i % half_rows // 2) + 2 * (i // half_rows) + i % 2)
    for a, grad in enumerate((dq * FACTOR, dk * FACTOR, dv)):
        sorted_rows = dot(order, grad.astype(BF)).astype(BF)
        for b in range(2):
            low = HD * (3 * b + a)
            out_ref[:, low : low + HD] = sorted_rows[half_rows * b : half_rows * (b + 1)]
    i, j = iota((HD, HD), 0), iota((HD, HD), 1)
    order = choose(j == 18 * (i % 64 // 2) + 2 * (i // 64) + i % 2)
    out_t = dot_nt(order, out).astype(BF)
    for ref, half in ((keep_ref, core), (send_ref, 1 - core)):
        part = dot(out_t, dot(g, core_columns(half)).astype(BF)).astype(BF)
        for b in range(9):
            ref[:, HALF * b : HALF * (b + 1)] = part[64 * b : 64 * b + 64]


def on_device(query_s, key_s, value_s, query_t, key_t, value_t, grad_out, proj_s, proj_t):
    frames = lax.axis_size("frame")
    n_pix = lax.axis_size("pix")
    n_z = n_pix // 2
    pix = lax.axis_index("pix")
    core, z = pix % 2, pix // 2
    core_arg = core.reshape(1).astype(jnp.int32)
    core_swap = [(p, p ^ 1) for p in range(n_pix)]
    same_core = [[2 * i + c for i in range(n_z)] for c in range(2)]

    with jax.named_scope("spatial_grad_gather"):
        grad = grad_out[:, 0]
        own = lax.dynamic_index_in_dim(grad, core, 0, keepdims=False)
        other = lax.dynamic_index_in_dim(grad, 1 - core, 0, keepdims=False)
        other = lax.ppermute(other, "pix", core_swap)
        gathered = lax.all_gather(
            jnp.concatenate([own, other], 0), "pix", axis=0, axis_index_groups=same_core, tiled=True
        )

    with jax.named_scope("temporal_in"):
        flat = [a.reshape(128, a.shape[3]) for a in (query_t, key_t, value_t, grad_out)]
        sent_in = call(pack_time_kernel, 4, whole((frames, 4, 3 * HD + D), BF), 1)(*flat)
        moved_t = lax.all_to_all(sent_in, "frame", 0, 0, tiled=True).reshape(128, 3 * HD + D)

    with jax.named_scope("spatial_in"):
        flat = [a.reshape(128, HD) for a in (query_s, key_s, value_s)]
        packed = call(pack_kernel, 3, whole((n_pix, 64, 3 * HSIZE), BF), 1 << 26)(*flat)
        moved_s = lax.all_to_all(packed, "pix", 0, 0, tiled=True)

    with jax.named_scope("temporal_attention"):
        grads_t, keep_t, send_t = call(
            temporal_kernel,
            2,
            (whole((64, GRADS), BF), whole((64, SUMS_T), BF), whole((64, SUMS_T), BF)),
            1,
            scalars=1,
        )(core_arg, moved_t, proj_t)
        got_t = lax.ppermute(send_t, "pix", core_swap)
    with jax.named_scope("spatial_attention"):
        proj_h = lax.dynamic_slice_in_dim(proj_s, HSIZE * z, HSIZE, 0)
        proj_h = jnp.pad(proj_h, ((0, 128 - HSIZE), (0, 0)))
        grads_s, part_s = call(
            spatial_kernel,
            3,
            (whole((n_pix * 64, 3 * HSIZE), BF), whole((2 * frames, SUMS_S), BF)),
            1,
            scalars=1,
            scratch=[pltpu.VMEM((128, n_pix * 64), F32)] * 2 + [pltpu.VMEM((2 * frames, SUMS_S), F32)],
        )(core_arg, moved_s.reshape(n_pix * 64, 3 * HSIZE), gathered, proj_h)

    with jax.named_scope("temporal_out"):
        sent_out = call(merge_kernel, 4, whole((frames, 2, GRADS + SUMS_T + SUMS_S), BF), 1)(
            grads_t, keep_t, got_t, part_s
        )
        home_t = lax.all_to_all(sent_out, "frame", 0, 0, tiled=True)
        back = home_t[..., :GRADS].reshape(frames, 2, 2, 3, HD).transpose(3, 2, 1, 0, 4)
        outs_t = [back[a].reshape(2, 1, 64, HD) for a in range(3)]

    with jax.named_scope("spatial_projection"):
        sums_s = home_t[..., GRADS + SUMS_T :].astype(F32).sum(0).reshape(2, 9, 2, HSIZE)
        sums_s = sums_s.transpose(2, 1, 0, 3).reshape(2, 18, HSIZE)
        own_s = lax.dynamic_index_in_dim(sums_s, core, 0, keepdims=False)
        other_s = lax.dynamic_index_in_dim(sums_s, 1 - core, 0, keepdims=False)
        sums_s = own_s + lax.ppermute(other_s, "pix", core_swap)
        perm = []
        for y in range(8):
            for x in range(4):
                for zz in range(n_z):
                    for c in range(2):
                        source = (y * 4 + x) * n_pix + 2 * zz + c
                        perm.append((source, (zz * 4 + x) * n_pix + 2 * y + c))
        proj_s_grad = lax.ppermute(sums_s, ("frame", "pix"), perm)

    with jax.named_scope("temporal_projection"):
        sums_t = home_t[..., GRADS : GRADS + SUMS_T].astype(F32).sum(0).astype(BF)
        sums_t = sums_t.reshape(2, 9, n_z, HSIZE).transpose(2, 1, 0, 3).reshape(n_z, 36, 36)
        sums_t = jnp.pad(sums_t, ((0, 0), (0, 28), (0, 0)))
        sums_t = jnp.broadcast_to(sums_t[:, None], (n_z, 2, 64, 36)).reshape(n_pix, 64, 36)

    with jax.named_scope("spatial_out"):
        sent = jnp.concatenate([grads_s.reshape(n_pix, 64, 3 * HSIZE), sums_t], 2)
        home_s = lax.all_to_all(sent, "pix", 0, 0, tiled=True)
        outs_s = call(unpack_kernel, 1, (whole((128, HD), BF),) * 3, 1 << 26)(home_s)
        outs_s = [a.reshape(2, 1, 64, HD) for a in outs_s]
        last_t = home_s[:, :36, 3 * HSIZE :].reshape(n_z, 2, 36, 36)
        last_t = lax.dynamic_index_in_dim(last_t, core, 1, keepdims=False)
        proj_t_grad = last_t.astype(F32).sum(0).reshape(18, HSIZE)

    return (*outs_s, *outs_t, proj_s_grad, proj_t_grad)


def solution(mesh):
    rows = P(None, "frame", "pix", None)
    out_specs = (rows,) * 6 + (P("frame", "pix"),) * 2
    return jax.shard_map(
        on_device,
        mesh=mesh,
        in_specs=(rows,) * 7 + (P(), P()),
        out_specs=out_specs,
        check_vma=False,
    )
```

```python
import jax
import jax.numpy as jnp
from jax import lax
from jax.experimental import pallas as pl
from jax.experimental.pallas import tpu as pltpu
from jax.sharding import PartitionSpec as P

HSIZE = 72
HEADS = 8
HD = 576
D = 1152
HALF = 576
GRADS = 6 * HD
SUMS_T = 9 * HALF
SUMS_S = 9 * 2 * HSIZE
THREE = 3 * HSIZE
FACTOR = HSIZE ** (-0.5)
BF = jnp.bfloat16
F32 = jnp.float32


def dot(a, b):
    return lax.dot_general(a, b, (((1,), (0,)), ((), ())), preferred_element_type=F32)


def dot_nt(a, b):
    return lax.dot_general(a, b, (((1,), (1,)), ((), ())), preferred_element_type=F32)


def iota(shape, dim):
    return lax.broadcasted_iota(jnp.int32, shape, dim)


def choose(cond):
    return jnp.where(cond, 1.0, 0.0).astype(BF)


def window(h):
    start = (HSIZE * h) // 128 * 128
    return start, min(256, HD - start), HSIZE * h - start


def core_columns(core):
    col = iota((D, HALF), 1)
    z = col // HSIZE
    return choose(iota((D, HALF), 0) == col + HSIZE * z + HSIZE * core)


def whole(shape, dtype):
    return jax.ShapeDtypeStruct(shape, dtype)


def call(kernel, n_in, out_shape, scalars=0, scratch=(), anywhere=0, mib=32):
    many = isinstance(out_shape, (tuple, list))
    vmem = pl.BlockSpec(memory_space=pltpu.VMEM)
    source = pl.BlockSpec(memory_space=pl.ANY)
    smem = pl.BlockSpec(memory_space=pltpu.SMEM)
    return pl.pallas_call(
        kernel,
        out_shape=out_shape,
        in_specs=[smem] * scalars + [vmem] * n_in + [source] * anywhere,
        out_specs=[vmem] * len(out_shape) if many else vmem,
        scratch_shapes=list(scratch),
        compiler_params=pltpu.CompilerParams(vmem_limit_bytes=mib * 1024 * 1024),
        cost_estimate=pl.CostEstimate(flops=1, bytes_accessed=1, transcendentals=0),
    )


def pack_kernel(q_ref, k_ref, v_ref, out_ref):
    for h in range(HEADS):
        start, width, offset = window(h)
        total = None
        for a, ref in enumerate((q_ref, k_ref, v_ref)):
            i, j = iota((width, 256), 0), iota((width, 256), 1) - HSIZE * a
            sel = choose((i - offset == j) & (j >= 0) & (j < HSIZE))
            part = dot(ref[:, start : start + width], sel)
            total = part if total is None else total + part
        total = total.astype(BF)[:, :THREE]
        for c in range(2):
            for n in range(4):
                low = 64 * c + 16 * n
                out_ref[2 * h + c, :, THREE * n : THREE * (n + 1)] = total[low : low + 16]


def ride_kernel(home_ref, grads_ref, out_ref, rows_ref):
    out_ref[...] = grads_ref[...]
    total = None
    for f in range(home_ref.shape[0]):
        part = home_ref[f, :, GRADS : GRADS + SUMS_T].astype(F32)
        total = part if total is None else total + part
    for z in range(out_ref.shape[0] // 2):
        for b in range(9):
            low = HALF * b + HSIZE * z
            rows_ref[z, 2 * b : 2 * b + 2] = total[:, low : low + HSIZE]
        for n in range(2):
            half = rows_ref[z, :, 36 * n : 36 * (n + 1)].astype(BF)
            for c in range(2):
                out_ref[2 * z + c, 32 * n : 32 * n + 18, THREE:] = half


def unpack_kernel(place_ref, x_ref, dq_ref, dk_ref, dv_ref, sum_ref):
    core = place_ref[0]
    for n in range(2):
        total = None
        for z in range(x_ref.shape[0] // 2):
            part = x_ref[2 * z + core, 32 * n : 32 * n + 18, THREE:].astype(F32)
            total = part if total is None else total + part
        sum_ref[:, 36 * n : 36 * (n + 1)] = total
    for a, ref in enumerate((dq_ref, dk_ref, dv_ref)):
        for start in range(0, HD, 128):
            width = min(128, HD - start)
            total = None
            for h in range(HEADS):
                low = HSIZE * h - start
                if low >= width or low + HSIZE <= 0:
                    continue
                pair = jnp.concatenate([x_ref[2 * h], x_ref[2 * h + 1]], 0)[:, :THREE]
                i, j = iota((THREE, width), 0) - HSIZE * a, iota((THREE, width), 1)
                sel = choose((i + low == j) & (i >= 0) & (i < HSIZE))
                part = dot(pair, sel)
                total = part if total is None else total + part
            ref[:, start : start + width] = total.astype(BF)


def split_heads(x_ref):
    sources, tall = x_ref.shape[0], x_ref.shape[1]
    i, j = iota((THREE, 384), 0), iota((THREE, 384), 1)
    sel = choose((i == HSIZE * (j // 128) + j % 128) & (j % 128 < HSIZE))
    blocks = [
        dot(x_ref[:, :, THREE * n : THREE * (n + 1)].reshape(sources * tall, THREE), sel)
        for n in range(x_ref.shape[2] // THREE)
    ]
    keys = jnp.concatenate([part[:, 128:256] for part in blocks], 0).astype(BF)
    values = jnp.concatenate([part[:, 256:] for part in blocks], 0).astype(BF)
    return sel, blocks, keys, values


def attend_block(queries, keys, values):
    scores = dot_nt(queries.astype(BF), keys) * FACTOR
    e = jnp.exp(scores - scores.max(-1, keepdims=True))
    inverse = 1.0 / e.sum(-1, keepdims=True)
    return e, inverse, (dot(e.astype(BF), values) * inverse).astype(BF)


def forward_kernel(
    place_ref, x_ref, got_ref, grads_any, g_any, keep_any, out_ref, chunk_ref, g_ref, keep_ref, sems
):
    core = place_ref[0]
    copies = [
        pltpu.make_async_copy(keep_any, keep_ref, sems.at[0]),
        pltpu.make_async_copy(g_any, g_ref, sems.at[1]),
        pltpu.make_async_copy(grads_any, out_ref.at[:, :, :GRADS], sems.at[2]),
    ]
    for copy in copies:
        copy.start()
    n_z = g_ref.shape[0]
    _, blocks, keys, values = split_heads(x_ref)
    pairs = []
    for part in blocks:
        out = attend_block(part[:, :128], keys, values)[2].astype(F32)
        pairs.append(out.reshape(n_z, 2, 16, 128))
    copies[0].wait()
    total = (keep_ref[...].astype(F32) + got_ref[...].astype(F32)).astype(BF)
    for f in range(out_ref.shape[0]):
        rows = slice(2 * f, 2 * f + 2)
        out_ref[f, :, GRADS : GRADS + SUMS_T] = total[rows]
    even = jnp.concatenate([pair[:, 0] for pair in pairs], 1)
    odd = jnp.concatenate([pair[:, 1] for pair in pairs], 1)
    sums = None
    copies[1].wait()
    for n, tokens in enumerate((jnp.where(core == 0, even, odd), jnp.where(core == 0, odd, even))):
        rows = n_z * 64
        term = dot(tokens.reshape(rows, 128).T.astype(BF), g_ref[:, n].reshape(rows, D))
        sums = term if sums is None else sums + term
    i, j = iota((HSIZE, 128), 0), iota((HSIZE, 128), 1)
    sums = dot(choose(j == 18 * (i % 8 // 2) + 2 * (i // 8) + i % 2), sums.astype(BF))
    wide = 2 * HSIZE
    for y in range(8):
        columns = sums[:, wide * y : wide * (y + 1)]
        for b in range(9):
            chunk_ref[8 * y : 8 * (y + 1), wide * b : wide * (b + 1)] = columns[8 * b : 8 * (b + 1)]
    chunks = chunk_ref[...].astype(BF)
    for f in range(out_ref.shape[0]):
        out_ref[f, :, GRADS + SUMS_T :] = chunks[2 * f : 2 * f + 2]
    copies[2].wait()


def backward_kernel(place_ref, x_ref, g_ref, proj_ref, out_ref, dkt_ref, dvt_ref):
    core = place_ref[0]
    n_z = g_ref.shape[0]
    sel, blocks, keys, values = split_heads(x_ref)
    own, other = [
        dot_nt(g_ref[:, n].reshape(n_z * 64, D), proj_ref[...]).reshape(n_z, 64, 128)
        for n in range(2)
    ]
    even, odd = jnp.where(core == 0, own, other), jnp.where(core == 0, other, own)
    grads = jnp.concatenate([even[:, None], odd[:, None]], 1).astype(BF).astype(F32)
    step = 2 * n_z * 16
    dqs = []
    for n, part in enumerate(blocks):
        q, do = part[:, :128], grads[:, :, 16 * n : 16 * (n + 1)].reshape(step, 128)
        e, inverse, out = attend_block(q, keys, values)
        weights = e * inverse
        delta = (do * out.astype(F32)).sum(-1, keepdims=True)
        dprob = dot_nt(do.astype(BF), values)
        dscore = (weights * (dprob - delta)).astype(BF)
        dqs.append((dot(dscore, keys) * FACTOR).astype(BF))
        dkt = dot(q.T.astype(BF), dscore)
        dvt = dot(do.T.astype(BF), weights.astype(BF))
        if n == 0:
            dkt_ref[...] = dkt
            dvt_ref[...] = dvt
        else:
            dkt_ref[...] += dkt
            dvt_ref[...] += dvt
    out_ref[:, :, THREE:] = jnp.zeros((2 * n_z, 64, 36), BF)
    for n in range(len(blocks)):
        rows = slice(step * n, step * (n + 1))
        dk = (dkt_ref[:, rows].T * FACTOR).astype(BF)
        dv = dvt_ref[:, rows].T.astype(BF)
        back = dot_nt(jnp.concatenate([dqs[n], dk, dv], 1), sel).astype(BF)
        out_ref[:, 16 * n : 16 * (n + 1), :THREE] = back.reshape(2 * n_z, 16, THREE)


def pack_time_kernel(q_ref, k_ref, v_ref, g_ref, out_ref):
    rows, frames = q_ref.shape[0], out_ref.shape[0]
    group = rows // frames
    i, j = iota((rows, rows), 0), iota((rows, rows), 1)
    order = choose(j == frames * (i % group) + i // group)
    moved = [dot(order, ref[...]).astype(BF) for ref in (q_ref, k_ref, v_ref, g_ref)]
    moved = jnp.concatenate(moved, 1)
    for f in range(frames):
        out_ref[f] = moved[group * f : group * (f + 1)]


def add_tiles(tiles, start, part):
    for low in range(0, part.shape[1], 128):
        piece = part[:, low : low + 128]
        n = (start + low) // 128
        tiles[n] = tiles[n] + piece if n in tiles else piece


def joined(tiles):
    return jnp.concatenate([tiles[n] for n in sorted(tiles)], 1)


def temporal_kernel(place_ref, x_ref, proj_any, out_ref, keep_ref, send_ref, proj_ref, sem):
    core = place_ref[0]
    copy = pltpu.make_async_copy(proj_any, proj_ref, sem)
    copy.start()
    rows = x_ref.shape[0]
    group = 4
    q, k, v = [x_ref[:, HD * a : HD * (a + 1)] for a in range(3)]
    g = x_ref[:, 3 * HD :]
    same = iota((rows, rows), 0) % group == iota((rows, rows), 1) % group
    views = []
    for h in range(HEADS):
        start, width, offset = window(h)
        lane = iota((1, width), 1)
        mask = choose((lane >= offset) & (lane < offset + HSIZE))
        views.append((start, slice(start, start + width), mask))
    weights = []
    tiles = {}
    for start, cols, mask in views:
        scores = jnp.where(same, dot_nt(q[:, cols] * mask, k[:, cols]) * FACTOR, -1e30)
        e = jnp.where(same, jnp.exp(scores - scores.max(-1, keepdims=True)), 0.0)
        inverse = 1.0 / e.sum(-1, keepdims=True)
        add_tiles(tiles, start, dot(e.astype(BF), v[:, cols] * mask) * inverse)
        weights.append(e * inverse)
    out = joined(tiles).astype(BF)
    copy.wait()
    do = dot_nt(g, proj_ref[...]).astype(BF)
    product = do.astype(F32) * out.astype(F32)
    dqs, dks, dvs = {}, {}, {}
    for weight, (start, cols, mask) in zip(weights, views):
        dom = do[:, cols] * mask
        delta = (product[:, cols] * mask.astype(F32)).sum(-1, keepdims=True)
        dscore = weight * (dot_nt(dom, v[:, cols]) - delta)
        add_tiles(dqs, start, dot(dscore.astype(BF), k[:, cols] * mask))
        add_tiles(dks, start, dot(dscore.T.astype(BF), q[:, cols] * mask))
        add_tiles(dvs, start, dot(weight.T.astype(BF), dom))
    dq, dk, dv = joined(dqs), joined(dks), joined(dvs)
    i, j = iota((rows, rows), 0), iota((rows, rows), 1)
    half_rows = rows // 2
    order = choose(j == group * (i % half_rows // 2) + 2 * (i // half_rows) + i % 2)
    for a, grad in enumerate((dq * FACTOR, dk * FACTOR, dv)):
        sorted_rows = dot(order, grad.astype(BF)).astype(BF)
        for b in range(2):
            low = HD * (3 * b + a)
            for f in range(out_ref.shape[0]):
                row = half_rows * b + 2 * f
                out_ref[f, :, low : low + HD] = sorted_rows[row : row + 2]
    i, j = iota((HD, HD), 0), iota((HD, HD), 1)
    order = choose(j == 18 * (i % 64 // 2) + 2 * (i // 64) + i % 2)
    out_t = dot_nt(order, out).astype(BF)
    for ref, half in ((keep_ref, core), (send_ref, 1 - core)):
        part = dot(out_t, dot(g, core_columns(half)).astype(BF)).astype(BF)
        for b in range(9):
            ref[:, HALF * b : HALF * (b + 1)] = part[64 * b : 64 * b + 64]


def on_device(query_s, key_s, value_s, query_t, key_t, value_t, grad_out, proj_s, proj_t):
    frames = lax.axis_size("frame")
    n_pix = lax.axis_size("pix")
    n_z = n_pix // 2
    pix = lax.axis_index("pix")
    core, z = pix % 2, pix // 2
    place = jnp.stack([core, z]).astype(jnp.int32)
    core_swap = [(p, p ^ 1) for p in range(n_pix)]
    same_core = [[2 * i + c for i in range(n_z)] for c in range(2)]

    with jax.named_scope("temporal_in"):
        flat = [a.reshape(128, a.shape[3]) for a in (query_t, key_t, value_t, grad_out)]
        sent_in = call(pack_time_kernel, 4, whole((frames, 4, 3 * HD + D), BF))(*flat)
        moved_t = lax.all_to_all(sent_in, "frame", 0, 0, tiled=True).reshape(128, 3 * HD + D)

    with jax.named_scope("spatial_grad_gather"):
        grad = grad_out[:, 0]
        own = lax.dynamic_index_in_dim(grad, core, 0, keepdims=False)
        other = lax.dynamic_index_in_dim(grad, 1 - core, 0, keepdims=False)
        other = lax.ppermute(other, "pix", core_swap)
        gathered = lax.all_gather(
            jnp.concatenate([own, other], 0), "pix", axis=0, axis_index_groups=same_core, tiled=True
        ).reshape(n_z, 2, 64, D)

    with jax.named_scope("spatial_in"):
        flat = [a.reshape(128, HD) for a in (query_s, key_s, value_s)]
        packed = call(pack_kernel, 3, whole((n_pix, 16, 4 * THREE), BF))(*flat)
        moved_s = lax.all_to_all(packed, "pix", 0, 0, tiled=True)

    with jax.named_scope("temporal_attention"):
        grads_t, keep_t, send_t = call(
            temporal_kernel,
            1,
            (whole((frames, 2, GRADS), BF), whole((64, SUMS_T), BF), whole((64, SUMS_T), BF)),
            scalars=1,
            scratch=[pltpu.VMEM((HD, D), BF), pltpu.SemaphoreType.DMA],
            anywhere=1,
        )(place, moved_t, proj_t)
        got_t = lax.ppermute(send_t, "pix", core_swap)

    with jax.named_scope("spatial_forward"):
        sent_out = call(
            forward_kernel,
            2,
            whole((frames, 2, GRADS + SUMS_T + SUMS_S), BF),
            scalars=1,
            scratch=[
                pltpu.VMEM((2 * frames, SUMS_S), F32),
                pltpu.VMEM(gathered.shape, BF),
                pltpu.VMEM(keep_t.shape, BF),
                pltpu.SemaphoreType.DMA((3,)),
            ],
            anywhere=3,
            mib=56,
        )(place, moved_s, got_t, grads_t, gathered, keep_t)

    with jax.named_scope("temporal_out"):
        home_t = lax.all_to_all(sent_out, "frame", 0, 0, tiled=True)
        back = home_t[..., :GRADS].reshape(frames, 2, 2, 3, HD).transpose(3, 2, 1, 0, 4)
        outs_t = [back[a].reshape(2, 1, 64, HD) for a in range(3)]

    with jax.named_scope("spatial_backward"):
        proj_h = lax.dynamic_slice_in_dim(proj_s, HSIZE * z, HSIZE, 0)
        proj_h = jnp.pad(proj_h, ((0, 128 - HSIZE), (0, 0)))
        grads_s = call(
            backward_kernel,
            3,
            whole((n_pix, 64, THREE + 36), BF),
            scalars=1,
            scratch=[pltpu.VMEM((128, n_pix * 64), F32)] * 2,
        )(place, moved_s, gathered, proj_h)

    with jax.named_scope("spatial_projection"):
        sums_s = home_t[..., GRADS + SUMS_T :].astype(F32).sum(0).reshape(2, 9, 2, HSIZE)
        sums_s = sums_s.transpose(2, 1, 0, 3).reshape(2, 18, HSIZE)
        own_s = lax.dynamic_index_in_dim(sums_s, core, 0, keepdims=False)
        other_s = lax.dynamic_index_in_dim(sums_s, 1 - core, 0, keepdims=False)
        sums_s = own_s + lax.ppermute(other_s, "pix", core_swap)
        perm = []
        for y in range(8):
            for x in range(4):
                for zz in range(n_z):
                    for c in range(2):
                        source = (y * 4 + x) * n_pix + 2 * zz + c
                        perm.append((source, (zz * 4 + x) * n_pix + 2 * y + c))
        proj_s_grad = lax.ppermute(sums_s, ("frame", "pix"), perm)

    with jax.named_scope("spatial_out"):
        sent = call(
            ride_kernel,
            2,
            whole(grads_s.shape, BF),
            scratch=[pltpu.VMEM((n_z, 18, HSIZE), F32)],
        )(home_t, grads_s)
        home_s = lax.all_to_all(sent, "pix", 0, 0, tiled=True)
        *outs_s, proj_t_grad = call(
            unpack_kernel,
            1,
            (whole((128, HD), BF),) * 3 + (whole((18, HSIZE), F32),),
            scalars=1,
        )(place, home_s)
        outs_s = [a.reshape(2, 1, 64, HD) for a in outs_s]

    return (*outs_s, *outs_t, proj_s_grad, proj_t_grad)


def solution(mesh):
    rows = P(None, "frame", "pix", None)
    out_specs = (rows,) * 6 + (P("frame", "pix"),) * 2
    return jax.shard_map(
        on_device,
        mesh=mesh,
        in_specs=(rows,) * 7 + (P(), P()),
        out_specs=out_specs,
        check_vma=False,
    )
```

```python
import jax
import jax.numpy as jnp
from jax import lax
from jax.experimental import pallas as pl
from jax.experimental.pallas import tpu as pltpu
from jax.sharding import PartitionSpec as P

HSIZE = 72
HEADS = 8
HD = 576
D = 1152
HALF = 576
GRADS = 6 * HD
SUMS_T = 9 * HALF
SUMS_S = 9 * 2 * HSIZE
THREE = 3 * HSIZE
FACTOR = HSIZE ** (-0.5)
BF = jnp.bfloat16
F32 = jnp.float32


def dot(a, b):
    return lax.dot_general(a, b, (((1,), (0,)), ((), ())), preferred_element_type=F32)


def dot_nt(a, b):
    return lax.dot_general(a, b, (((1,), (1,)), ((), ())), preferred_element_type=F32)


def iota(shape, dim):
    return lax.broadcasted_iota(jnp.int32, shape, dim)


def choose(cond):
    return jnp.where(cond, 1.0, 0.0).astype(BF)


def window(h):
    start = (HSIZE * h) // 128 * 128
    return start, min(256, HD - start), HSIZE * h - start


def core_columns(core):
    col = iota((D, HALF), 1)
    z = col // HSIZE
    return choose(iota((D, HALF), 0) == col + HSIZE * z + HSIZE * core)


def whole(shape, dtype):
    return jax.ShapeDtypeStruct(shape, dtype)


def call(kernel, n_in, out_shape, scalars=0, scratch=(), anywhere=0, mib=32):
    many = isinstance(out_shape, (tuple, list))
    vmem = pl.BlockSpec(memory_space=pltpu.VMEM)
    source = pl.BlockSpec(memory_space=pl.ANY)
    smem = pl.BlockSpec(memory_space=pltpu.SMEM)
    return pl.pallas_call(
        kernel,
        out_shape=out_shape,
        in_specs=[smem] * scalars + [vmem] * n_in + [source] * anywhere,
        out_specs=[vmem] * len(out_shape) if many else vmem,
        scratch_shapes=list(scratch),
        compiler_params=pltpu.CompilerParams(vmem_limit_bytes=mib * 1024 * 1024),
        cost_estimate=pl.CostEstimate(flops=1, bytes_accessed=1, transcendentals=0),
    )


def pack_kernel(place_ref, q_ref, k_ref, v_ref, keep_ref, send_ref):
    core = place_ref[0]
    for h in range(HEADS):
        start, width, offset = window(h)
        total = None
        for a, ref in enumerate((q_ref, k_ref, v_ref)):
            i, j = iota((width, 256), 0), iota((width, 256), 1) - HSIZE * a
            sel = choose((i - offset == j) & (j >= 0) & (j < HSIZE))
            part = dot(ref[:, start : start + width], sel)
            total = part if total is None else total + part
        low, high = total[:64, :THREE], total[64:, :THREE]
        own = jnp.where(core == 0, low, high).astype(BF)
        other = jnp.where(core == 0, high, low).astype(BF)
        for n in range(4):
            cols, rows = slice(THREE * n, THREE * (n + 1)), slice(16 * n, 16 * (n + 1))
            keep_ref[h, :, cols] = own[rows]
            send_ref[h, :, cols] = other[rows]


def ride_kernel(home_ref, own_ref, got_ref, out_ref, rows_ref):
    out_ref[:, :64, :THREE] = own_ref[...]
    out_ref[:, 64:, :THREE] = got_ref[...]
    total = None
    for f in range(home_ref.shape[0]):
        part = home_ref[f, :, GRADS : GRADS + SUMS_T].astype(F32)
        total = part if total is None else total + part
    out_ref[:, :, THREE:] = jnp.zeros((out_ref.shape[0], 128, 36), BF)
    for z in range(out_ref.shape[0]):
        for b in range(9):
            low = HALF * b + HSIZE * z
            rows_ref[z, 2 * b : 2 * b + 2] = total[:, low : low + HSIZE]
        for n in range(2):
            half = rows_ref[z, :, 36 * n : 36 * (n + 1)].astype(BF)
            out_ref[z, 32 * n : 32 * n + 18, THREE:] = half


def unpack_kernel(place_ref, x_ref, dq_ref, dk_ref, dv_ref, sum_ref):
    core = place_ref[0]
    for n in range(2):
        total = None
        for z in range(x_ref.shape[0]):
            part = x_ref[z, 32 * n : 32 * n + 18, THREE:].astype(F32)
            total = part if total is None else total + part
        sum_ref[:, 36 * n : 36 * (n + 1)] = total
    for a, ref in enumerate((dq_ref, dk_ref, dv_ref)):
        for start in range(0, HD, 128):
            width = min(128, HD - start)
            total = None
            for h in range(HEADS):
                low = HSIZE * h - start
                if low >= width or low + HSIZE <= 0:
                    continue
                first, second = x_ref[h, :64, :THREE], x_ref[h, 64:, :THREE]
                pair = jnp.concatenate(
                    [jnp.where(core == 0, first, second), jnp.where(core == 0, second, first)], 0
                )
                i, j = iota((THREE, width), 0) - HSIZE * a, iota((THREE, width), 1)
                sel = choose((i + low == j) & (i >= 0) & (i < HSIZE))
                part = dot(pair, sel)
                total = part if total is None else total + part
            ref[:, start : start + width] = total.astype(BF)


def split_heads(x_ref):
    sources, tall = x_ref.shape[0], x_ref.shape[1]
    i, j = iota((THREE, 384), 0), iota((THREE, 384), 1)
    sel = choose((i == HSIZE * (j // 128) + j % 128) & (j % 128 < HSIZE))
    blocks = [
        dot(x_ref[:, :, THREE * n : THREE * (n + 1)].reshape(sources * tall, THREE), sel)
        for n in range(x_ref.shape[2] // THREE)
    ]
    keys = jnp.concatenate([part[:, 128:256] for part in blocks], 0).astype(BF)
    values = jnp.concatenate([part[:, 256:] for part in blocks], 0).astype(BF)
    return sel, blocks, keys, values


def attend_block(queries, keys, values):
    scores = dot_nt(queries.astype(BF), keys) * FACTOR
    e = jnp.exp(scores - scores.max(-1, keepdims=True))
    inverse = 1.0 / e.sum(-1, keepdims=True)
    return e, inverse, (dot(e.astype(BF), values) * inverse).astype(BF)


def forward_kernel(
    x_ref, got_ref, grads_any, g_any, keep_any, out_ref, chunk_ref, g_ref, keep_ref, sems
):
    copies = [
        pltpu.make_async_copy(keep_any, keep_ref, sems.at[0]),
        pltpu.make_async_copy(g_any, g_ref, sems.at[1]),
        pltpu.make_async_copy(grads_any, out_ref.at[:, :, :GRADS], sems.at[2]),
    ]
    for copy in copies:
        copy.start()
    n_z = g_ref.shape[0]
    _, blocks, keys, values = split_heads(x_ref)
    pairs = []
    for part in blocks:
        out = attend_block(part[:, :128], keys, values)[2].astype(F32)
        pairs.append(out.reshape(n_z, 2, 16, 128))
    copies[0].wait()
    total = (keep_ref[...].astype(F32) + got_ref[...].astype(F32)).astype(BF)
    for f in range(out_ref.shape[0]):
        rows = slice(2 * f, 2 * f + 2)
        out_ref[f, :, GRADS : GRADS + SUMS_T] = total[rows]
    own = jnp.concatenate([pair[:, 0] for pair in pairs], 1)
    other = jnp.concatenate([pair[:, 1] for pair in pairs], 1)
    sums = None
    copies[1].wait()
    for n, tokens in enumerate((own, other)):
        rows = n_z * 64
        term = dot(tokens.reshape(rows, 128).T.astype(BF), g_ref[:, n].reshape(rows, D))
        sums = term if sums is None else sums + term
    i, j = iota((HSIZE, 128), 0), iota((HSIZE, 128), 1)
    sums = dot(choose(j == 18 * (i % 8 // 2) + 2 * (i // 8) + i % 2), sums.astype(BF))
    wide = 2 * HSIZE
    for y in range(8):
        columns = sums[:, wide * y : wide * (y + 1)]
        for b in range(9):
            chunk_ref[8 * y : 8 * (y + 1), wide * b : wide * (b + 1)] = columns[8 * b : 8 * (b + 1)]
    chunks = chunk_ref[...].astype(BF)
    for f in range(out_ref.shape[0]):
        out_ref[f, :, GRADS + SUMS_T :] = chunks[2 * f : 2 * f + 2]
    copies[2].wait()


def backward_kernel(x_ref, g_ref, proj_ref, own_ref, other_ref, dkt_ref, dvt_ref):
    n_z = g_ref.shape[0]
    sel, blocks, keys, values = split_heads(x_ref)
    own, other = [
        dot_nt(g_ref[:, n].reshape(n_z * 64, D), proj_ref[...]).reshape(n_z, 64, 128)
        for n in range(2)
    ]
    grads = jnp.concatenate([own[:, None], other[:, None]], 1).astype(BF).astype(F32)
    step = 2 * n_z * 16
    dqs = []
    for n, part in enumerate(blocks):
        q, do = part[:, :128], grads[:, :, 16 * n : 16 * (n + 1)].reshape(step, 128)
        e, inverse, out = attend_block(q, keys, values)
        weights = e * inverse
        delta = (do * out.astype(F32)).sum(-1, keepdims=True)
        dprob = dot_nt(do.astype(BF), values)
        dscore = (weights * (dprob - delta)).astype(BF)
        dqs.append((dot(dscore, keys) * FACTOR).astype(BF))
        dkt = dot(q.T.astype(BF), dscore)
        dvt = dot(do.T.astype(BF), weights.astype(BF))
        if n == 0:
            dkt_ref[...] = dkt
            dvt_ref[...] = dvt
        else:
            dkt_ref[...] += dkt
            dvt_ref[...] += dvt
    for n in range(len(blocks)):
        rows = slice(step * n, step * (n + 1))
        dk = (dkt_ref[:, rows].T * FACTOR).astype(BF)
        dv = dvt_ref[:, rows].T.astype(BF)
        back = dot_nt(jnp.concatenate([dqs[n], dk, dv], 1), sel).astype(BF)
        back = back.reshape(n_z, 2, 16, THREE)
        own_ref[:, 16 * n : 16 * (n + 1)] = back[:, 0]
        other_ref[:, 16 * n : 16 * (n + 1)] = back[:, 1]


def pack_time_kernel(q_ref, k_ref, v_ref, g_ref, out_ref):
    rows, frames = q_ref.shape[0], out_ref.shape[0]
    group = rows // frames
    i, j = iota((rows, rows), 0), iota((rows, rows), 1)
    order = choose(j == frames * (i % group) + i // group)
    moved = [dot(order, ref[...]).astype(BF) for ref in (q_ref, k_ref, v_ref, g_ref)]
    moved = jnp.concatenate(moved, 1)
    for f in range(frames):
        out_ref[f] = moved[group * f : group * (f + 1)]


def add_tiles(tiles, start, part):
    for low in range(0, part.shape[1], 128):
        piece = part[:, low : low + 128]
        n = (start + low) // 128
        tiles[n] = tiles[n] + piece if n in tiles else piece


def joined(tiles):
    return jnp.concatenate([tiles[n] for n in sorted(tiles)], 1)


def temporal_kernel(place_ref, x_ref, proj_any, out_ref, keep_ref, send_ref, proj_ref, sem):
    core = place_ref[0]
    copy = pltpu.make_async_copy(proj_any, proj_ref, sem)
    copy.start()
    rows = x_ref.shape[0]
    group = 4
    q, k, v = [x_ref[:, HD * a : HD * (a + 1)] for a in range(3)]
    g = x_ref[:, 3 * HD :]
    same = iota((rows, rows), 0) % group == iota((rows, rows), 1) % group
    views = []
    for h in range(HEADS):
        start, width, offset = window(h)
        lane = iota((1, width), 1)
        mask = choose((lane >= offset) & (lane < offset + HSIZE))
        views.append((start, slice(start, start + width), mask))
    weights = []
    tiles = {}
    for start, cols, mask in views:
        scores = jnp.where(same, dot_nt(q[:, cols] * mask, k[:, cols]) * FACTOR, -1e30)
        e = jnp.where(same, jnp.exp(scores - scores.max(-1, keepdims=True)), 0.0)
        inverse = 1.0 / e.sum(-1, keepdims=True)
        add_tiles(tiles, start, dot(e.astype(BF), v[:, cols] * mask) * inverse)
        weights.append(e * inverse)
    out = joined(tiles).astype(BF)
    copy.wait()
    do = dot_nt(g, proj_ref[...]).astype(BF)
    product = do.astype(F32) * out.astype(F32)
    dqs, dks, dvs = {}, {}, {}
    for weight, (start, cols, mask) in zip(weights, views):
        dom = do[:, cols] * mask
        delta = (product[:, cols] * mask.astype(F32)).sum(-1, keepdims=True)
        dscore = weight * (dot_nt(dom, v[:, cols]) - delta)
        add_tiles(dqs, start, dot(dscore.astype(BF), k[:, cols] * mask))
        add_tiles(dks, start, dot(dscore.T.astype(BF), q[:, cols] * mask))
        add_tiles(dvs, start, dot(weight.T.astype(BF), dom))
    dq, dk, dv = joined(dqs), joined(dks), joined(dvs)
    i, j = iota((rows, rows), 0), iota((rows, rows), 1)
    half_rows = rows // 2
    order = choose(j == group * (i % half_rows // 2) + 2 * (i // half_rows) + i % 2)
    for a, grad in enumerate((dq * FACTOR, dk * FACTOR, dv)):
        sorted_rows = dot(order, grad.astype(BF)).astype(BF)
        for b in range(2):
            low = HD * (3 * b + a)
            for f in range(out_ref.shape[0]):
                row = half_rows * b + 2 * f
                out_ref[f, :, low : low + HD] = sorted_rows[row : row + 2]
    i, j = iota((HD, HD), 0), iota((HD, HD), 1)
    order = choose(j == 18 * (i % 64 // 2) + 2 * (i // 64) + i % 2)
    out_t = dot_nt(order, out).astype(BF)
    for ref, half in ((keep_ref, core), (send_ref, 1 - core)):
        part = dot(out_t, dot(g, core_columns(half)).astype(BF)).astype(BF)
        for b in range(9):
            ref[:, HALF * b : HALF * (b + 1)] = part[64 * b : 64 * b + 64]


def on_device(query_s, key_s, value_s, query_t, key_t, value_t, grad_out, proj_s, proj_t):
    frames = lax.axis_size("frame")
    n_pix = lax.axis_size("pix")
    n_z = n_pix // 2
    pix = lax.axis_index("pix")
    core, z = pix % 2, pix // 2
    place = jnp.stack([core, z]).astype(jnp.int32)
    core_swap = [(p, p ^ 1) for p in range(n_pix)]
    same_core = [[2 * i + c for i in range(n_z)] for c in range(2)]

    with jax.named_scope("temporal_in"):
        flat = [a.reshape(128, a.shape[3]) for a in (query_t, key_t, value_t, grad_out)]
        sent_in = call(pack_time_kernel, 4, whole((frames, 4, 3 * HD + D), BF))(*flat)
        moved_t = lax.all_to_all(sent_in, "frame", 0, 0, tiled=True).reshape(128, 3 * HD + D)

    with jax.named_scope("spatial_grad_gather"):
        grad = grad_out[:, 0]
        own = lax.dynamic_index_in_dim(grad, core, 0, keepdims=False)
        other = lax.dynamic_index_in_dim(grad, 1 - core, 0, keepdims=False)
        other = lax.ppermute(other, "pix", core_swap)
        gathered = lax.all_gather(
            jnp.concatenate([own, other], 0), "pix", axis=0, axis_index_groups=same_core, tiled=True
        ).reshape(n_z, 2, 64, D)

    with jax.named_scope("spatial_in"):
        flat = [a.reshape(128, HD) for a in (query_s, key_s, value_s)]
        keep_s, send_s = call(
            pack_kernel, 3, (whole((n_z, 16, 4 * THREE), BF),) * 2, scalars=1
        )(place, *flat)
        packed = jnp.concatenate([keep_s, lax.ppermute(send_s, "pix", core_swap)], 1)
        moved_s = lax.all_to_all(packed, "pix", 0, 0, axis_index_groups=same_core, tiled=True)

    with jax.named_scope("temporal_attention"):
        grads_t, keep_t, send_t = call(
            temporal_kernel,
            1,
            (whole((frames, 2, GRADS), BF), whole((64, SUMS_T), BF), whole((64, SUMS_T), BF)),
            scalars=1,
            scratch=[pltpu.VMEM((HD, D), BF), pltpu.SemaphoreType.DMA],
            anywhere=1,
            mib=56,
        )(place, moved_t, proj_t)
        got_t = lax.ppermute(send_t, "pix", core_swap)

    with jax.named_scope("spatial_forward"):
        sent_out = call(
            forward_kernel,
            2,
            whole((frames, 2, GRADS + SUMS_T + SUMS_S), BF),
            scratch=[
                pltpu.VMEM((2 * frames, SUMS_S), F32),
                pltpu.VMEM(gathered.shape, BF),
                pltpu.VMEM(keep_t.shape, BF),
                pltpu.SemaphoreType.DMA((3,)),
            ],
            anywhere=3,
            mib=56,
        )(moved_s, got_t, grads_t, gathered, keep_t)

    with jax.named_scope("temporal_out"):
        home_t = lax.all_to_all(sent_out, "frame", 0, 0, tiled=True)
        back = home_t[..., :GRADS].reshape(frames, 2, 2, 3, HD).transpose(3, 2, 1, 0, 4)
        outs_t = [back[a].reshape(2, 1, 64, HD) for a in range(3)]

    with jax.named_scope("spatial_backward"):
        proj_h = lax.dynamic_slice_in_dim(proj_s, HSIZE * z, HSIZE, 0)
        proj_h = jnp.pad(proj_h, ((0, 128 - HSIZE), (0, 0)))
        own_s, other_s = call(
            backward_kernel,
            3,
            (whole((n_z, 64, THREE), BF),) * 2,
            scratch=[pltpu.VMEM((128, n_pix * 64), F32)] * 2,
        )(moved_s, gathered, proj_h)

        got_s = lax.ppermute(other_s, "pix", core_swap)

    with jax.named_scope("spatial_projection"):
        sums_s = home_t[..., GRADS + SUMS_T :].astype(F32).sum(0).reshape(2, 9, 2, HSIZE)
        sums_s = sums_s.transpose(2, 1, 0, 3).reshape(2, 18, HSIZE)
        own_sums = lax.dynamic_index_in_dim(sums_s, core, 0, keepdims=False)
        other_sums = lax.dynamic_index_in_dim(sums_s, 1 - core, 0, keepdims=False)
        sums_s = own_sums + lax.ppermute(other_sums, "pix", core_swap)
        perm = []
        for y in range(8):
            for x in range(4):
                for zz in range(n_z):
                    for c in range(2):
                        source = (y * 4 + x) * n_pix + 2 * zz + c
                        perm.append((source, (zz * 4 + x) * n_pix + 2 * y + c))
        proj_s_grad = lax.ppermute(sums_s, ("frame", "pix"), perm)

    with jax.named_scope("spatial_out"):
        sent = call(
            ride_kernel,
            3,
            whole((n_z, 128, THREE + 36), BF),
            scratch=[pltpu.VMEM((n_z, 18, HSIZE), F32)],
        )(home_t, own_s, got_s)
        home_s = lax.all_to_all(sent, "pix", 0, 0, axis_index_groups=same_core, tiled=True)
        *outs_s, proj_t_grad = call(
            unpack_kernel,
            1,
            (whole((128, HD), BF),) * 3 + (whole((18, HSIZE), F32),),
            scalars=1,
        )(place, home_s)
        outs_s = [a.reshape(2, 1, 64, HD) for a in outs_s]

    return (*outs_s, *outs_t, proj_s_grad, proj_t_grad)


def solution(mesh):
    rows = P(None, "frame", "pix", None)
    out_specs = (rows,) * 6 + (P("frame", "pix"),) * 2
    return jax.shard_map(
        on_device,
        mesh=mesh,
        in_specs=(rows,) * 7 + (P(), P()),
        out_specs=out_specs,
        check_vma=False,
    )
```

```python
import jax
import jax.numpy as jnp
from jax import lax
from jax.experimental import pallas as pl
from jax.experimental.pallas import tpu as pltpu
from jax.sharding import PartitionSpec as P

HSIZE = 72
HEADS = 8
HD = 576
D = 1152
HALF = 576
GRADS = 6 * HD
SUMS_T = 9 * HALF
SUMS_S = 9 * 2 * HSIZE
THREE = 3 * HSIZE
FACTOR = HSIZE ** (-0.5)
FACTOR_LOG2 = FACTOR * 1.4426950408889634
BF = jnp.bfloat16
F32 = jnp.float32


def dot(a, b):
    return lax.dot_general(a, b, (((1,), (0,)), ((), ())), preferred_element_type=F32)


def dot_nt(a, b):
    return lax.dot_general(a, b, (((1,), (1,)), ((), ())), preferred_element_type=F32)


def iota(shape, dim):
    return lax.broadcasted_iota(jnp.int32, shape, dim)


def choose(cond):
    return jnp.where(cond, 1.0, 0.0).astype(BF)


def window(h):
    start = (HSIZE * h) // 128 * 128
    return start, min(256, HD - start), HSIZE * h - start


def core_columns(core):
    col = iota((D, HALF), 1)
    z = col // HSIZE
    return choose(iota((D, HALF), 0) == col + HSIZE * z + HSIZE * core)


def whole(shape, dtype):
    return jax.ShapeDtypeStruct(shape, dtype)


def call(kernel, n_in, out_shape, scalars=0, scratch=(), anywhere=0, mib=32):
    many = isinstance(out_shape, (tuple, list))
    vmem = pl.BlockSpec(memory_space=pltpu.VMEM)
    source = pl.BlockSpec(memory_space=pl.ANY)
    smem = pl.BlockSpec(memory_space=pltpu.SMEM)
    return pl.pallas_call(
        kernel,
        out_shape=out_shape,
        in_specs=[smem] * scalars + [vmem] * n_in + [source] * anywhere,
        out_specs=[vmem] * len(out_shape) if many else vmem,
        scratch_shapes=list(scratch),
        compiler_params=pltpu.CompilerParams(vmem_limit_bytes=mib * 1024 * 1024),
        cost_estimate=pl.CostEstimate(flops=1, bytes_accessed=1, transcendentals=0),
    )


def pack_kernel(place_ref, q_ref, k_ref, v_ref, keep_ref, send_ref):
    core = place_ref[0]
    for h in range(HEADS):
        start, width, offset = window(h)
        total = None
        for a, ref in enumerate((q_ref, k_ref, v_ref)):
            i, j = iota((width, 256), 0), iota((width, 256), 1) - HSIZE * a
            sel = choose((i - offset == j) & (j >= 0) & (j < HSIZE))
            part = dot(ref[:, start : start + width], sel)
            total = part if total is None else total + part
        low, high = total[:64, :THREE], total[64:, :THREE]
        own = jnp.where(core == 0, low, high).astype(BF)
        other = jnp.where(core == 0, high, low).astype(BF)
        for n in range(4):
            cols, rows = slice(THREE * n, THREE * (n + 1)), slice(16 * n, 16 * (n + 1))
            keep_ref[h, :, cols] = own[rows]
            send_ref[h, :, cols] = other[rows]


def ride_kernel(home_ref, own_ref, got_ref, out_ref, rows_ref):
    out_ref[:, :64, :THREE] = own_ref[...]
    out_ref[:, 64:, :THREE] = got_ref[...]
    total = None
    for f in range(home_ref.shape[0]):
        part = home_ref[f, :, GRADS : GRADS + SUMS_T].astype(F32)
        total = part if total is None else total + part
    out_ref[:, :, THREE:] = jnp.zeros((out_ref.shape[0], 128, 36), BF)
    for z in range(out_ref.shape[0]):
        for b in range(9):
            low = HALF * b + HSIZE * z
            rows_ref[z, 2 * b : 2 * b + 2] = total[:, low : low + HSIZE]
        for n in range(2):
            half = rows_ref[z, :, 36 * n : 36 * (n + 1)].astype(BF)
            out_ref[z, 32 * n : 32 * n + 18, THREE:] = half


def unpack_kernel(place_ref, x_ref, other_ref, dq_ref, dk_ref, dv_ref, sum_ref, other_out_ref):
    core = place_ref[0]
    other_out_ref[...] = other_ref[...]
    for n in range(2):
        total = None
        for z in range(x_ref.shape[0]):
            part = x_ref[z, 32 * n : 32 * n + 18, THREE:].astype(F32)
            total = part if total is None else total + part
        sum_ref[:, 36 * n : 36 * (n + 1)] = total
    for a, ref in enumerate((dq_ref, dk_ref, dv_ref)):
        for start in range(0, HD, 128):
            width = min(128, HD - start)
            total = None
            for h in range(HEADS):
                low = HSIZE * h - start
                if low >= width or low + HSIZE <= 0:
                    continue
                first, second = x_ref[h, :64, :THREE], x_ref[h, 64:, :THREE]
                pair = jnp.concatenate(
                    [jnp.where(core == 0, first, second), jnp.where(core == 0, second, first)], 0
                )
                i, j = iota((THREE, width), 0) - HSIZE * a, iota((THREE, width), 1)
                sel = choose((i + low == j) & (i >= 0) & (i < HSIZE))
                part = dot(pair, sel)
                total = part if total is None else total + part
            ref[:, start : start + width] = total.astype(BF)


def split_heads(x_ref):
    sources, tall = x_ref.shape[0], x_ref.shape[1]
    i, j = iota((THREE, 384), 0), iota((THREE, 384), 1)
    sel = choose((i == HSIZE * (j // 128) + j % 128) & (j % 128 < HSIZE))
    blocks = [
        dot(x_ref[:, :, THREE * n : THREE * (n + 1)].reshape(sources * tall, THREE), sel)
        for n in range(x_ref.shape[2] // THREE)
    ]
    keys = jnp.concatenate([part[:, 128:256] for part in blocks], 0).astype(BF)
    values = jnp.concatenate([part[:, 256:] for part in blocks], 0).astype(BF)
    return sel, blocks, keys, values


def attend_block(queries, keys, values):
    scores = dot_nt(queries.astype(BF), keys)
    e = jnp.exp2((scores - scores.max(-1, keepdims=True)) * FACTOR_LOG2)
    inverse = 1.0 / e.sum(-1, keepdims=True)
    return e, inverse, (dot(e.astype(BF), values) * inverse).astype(BF)


def forward_kernel(
    x_ref, got_ref, grads_any, g_any, keep_any, out_ref, chunk_ref, g_ref, keep_ref, sems
):
    copies = [
        pltpu.make_async_copy(keep_any, keep_ref, sems.at[0]),
        pltpu.make_async_copy(g_any, g_ref, sems.at[1]),
        pltpu.make_async_copy(grads_any, out_ref.at[:, :, :GRADS], sems.at[2]),
    ]
    for copy in copies:
        copy.start()
    n_z = g_ref.shape[0]
    _, blocks, keys, values = split_heads(x_ref)
    pairs = []
    for part in blocks:
        out = attend_block(part[:, :128], keys, values)[2].astype(F32)
        pairs.append(out.reshape(n_z, 2, 16, 128))
    copies[0].wait()
    total = (keep_ref[...].astype(F32) + got_ref[...].astype(F32)).astype(BF)
    for f in range(out_ref.shape[0]):
        rows = slice(2 * f, 2 * f + 2)
        out_ref[f, :, GRADS : GRADS + SUMS_T] = total[rows]
    own = jnp.concatenate([pair[:, 0] for pair in pairs], 1)
    other = jnp.concatenate([pair[:, 1] for pair in pairs], 1)
    sums = None
    copies[1].wait()
    for n, tokens in enumerate((own, other)):
        rows = n_z * 64
        term = dot(tokens.reshape(rows, 128).T.astype(BF), g_ref[:, n].reshape(rows, D))
        sums = term if sums is None else sums + term
    i, j = iota((HSIZE, 128), 0), iota((HSIZE, 128), 1)
    sums = dot(choose(j == 18 * (i % 8 // 2) + 2 * (i // 8) + i % 2), sums.astype(BF))
    wide = 2 * HSIZE
    for y in range(8):
        columns = sums[:, wide * y : wide * (y + 1)]
        for b in range(9):
            chunk_ref[8 * y : 8 * (y + 1), wide * b : wide * (b + 1)] = columns[8 * b : 8 * (b + 1)]
    chunks = chunk_ref[...].astype(BF)
    for f in range(out_ref.shape[0]):
        out_ref[f, :, GRADS + SUMS_T :] = chunks[2 * f : 2 * f + 2]
    copies[2].wait()


def backward_kernel(x_ref, g_ref, proj_ref, own_ref, other_ref, dkt_ref, dvt_ref):
    n_z = g_ref.shape[0]
    sel, blocks, keys, values = split_heads(x_ref)
    own, other = [
        dot_nt(g_ref[:, n].reshape(n_z * 64, D), proj_ref[...]).reshape(n_z, 64, 128)
        for n in range(2)
    ]
    grads = jnp.concatenate([own[:, None], other[:, None]], 1).astype(BF).astype(F32)
    step = 2 * n_z * 16
    dqs = []
    for n, part in enumerate(blocks):
        q, do = part[:, :128], grads[:, :, 16 * n : 16 * (n + 1)].reshape(step, 128)
        e, inverse, out = attend_block(q, keys, values)
        weights = e * inverse
        delta = (do * out.astype(F32)).sum(-1, keepdims=True)
        dprob = dot_nt(do.astype(BF), values)
        dscore = (weights * (dprob - delta)).astype(BF)
        dqs.append((dot(dscore, keys) * FACTOR).astype(BF))
        dkt = dot(q.T.astype(BF), dscore)
        dvt = dot(do.T.astype(BF), weights.astype(BF))
        if n == 0:
            dkt_ref[...] = dkt
            dvt_ref[...] = dvt
        else:
            dkt_ref[...] += dkt
            dvt_ref[...] += dvt
    for n in range(len(blocks)):
        rows = slice(step * n, step * (n + 1))
        dk = (dkt_ref[:, rows].T * FACTOR).astype(BF)
        dv = dvt_ref[:, rows].T.astype(BF)
        back = dot_nt(jnp.concatenate([dqs[n], dk, dv], 1), sel).astype(BF)
        back = back.reshape(n_z, 2, 16, THREE)
        own_ref[:, 16 * n : 16 * (n + 1)] = back[:, 0]
        other_ref[:, 16 * n : 16 * (n + 1)] = back[:, 1]


def pack_time_kernel(q_ref, k_ref, v_ref, g_ref, out_ref):
    rows, frames = q_ref.shape[0], out_ref.shape[0]
    group = rows // frames
    i, j = iota((rows, rows), 0), iota((rows, rows), 1)
    order = choose(j == frames * (i % group) + i // group)
    moved = [dot(order, ref[...]).astype(BF) for ref in (q_ref, k_ref, v_ref, g_ref)]
    moved = jnp.concatenate(moved, 1)
    for f in range(frames):
        out_ref[f] = moved[group * f : group * (f + 1)]


def add_tiles(tiles, start, part):
    for low in range(0, part.shape[1], 128):
        piece = part[:, low : low + 128]
        n = (start + low) // 128
        tiles[n] = tiles[n] + piece if n in tiles else piece


def joined(tiles):
    return jnp.concatenate([tiles[n] for n in sorted(tiles)], 1)


def temporal_kernel(place_ref, x_ref, proj_any, out_ref, keep_ref, send_ref, proj_ref, sem):
    core = place_ref[0]
    copy = pltpu.make_async_copy(proj_any, proj_ref, sem)
    copy.start()
    rows = x_ref.shape[0]
    group = 4
    q, k, v = [x_ref[:, HD * a : HD * (a + 1)] for a in range(3)]
    g = x_ref[:, 3 * HD :]
    same = iota((rows, rows), 0) % group == iota((rows, rows), 1) % group
    views = []
    for h in range(HEADS):
        start, width, offset = window(h)
        lane = iota((1, width), 1)
        mask = choose((lane >= offset) & (lane < offset + HSIZE))
        views.append((start, slice(start, start + width), mask))
    weights = []
    tiles = {}
    for start, cols, mask in views:
        scores = jnp.where(same, dot_nt(q[:, cols] * mask, k[:, cols]) * FACTOR, -1e30)
        e = jnp.where(same, jnp.exp(scores - scores.max(-1, keepdims=True)), 0.0)
        inverse = 1.0 / e.sum(-1, keepdims=True)
        add_tiles(tiles, start, dot(e.astype(BF), v[:, cols] * mask) * inverse)
        weights.append(e * inverse)
    out = joined(tiles).astype(BF)
    copy.wait()
    do = dot_nt(g, proj_ref[...]).astype(BF)
    product = do.astype(F32) * out.astype(F32)
    dqs, dks, dvs = {}, {}, {}
    for weight, (start, cols, mask) in zip(weights, views):
        dom = do[:, cols] * mask
        delta = (product[:, cols] * mask.astype(F32)).sum(-1, keepdims=True)
        dscore = weight * (dot_nt(dom, v[:, cols]) - delta)
        add_tiles(dqs, start, dot(dscore.astype(BF), k[:, cols] * mask))
        add_tiles(dks, start, dot(dscore.T.astype(BF), q[:, cols] * mask))
        add_tiles(dvs, start, dot(weight.T.astype(BF), dom))
    dq, dk, dv = joined(dqs), joined(dks), joined(dvs)
    i, j = iota((rows, rows), 0), iota((rows, rows), 1)
    half_rows = rows // 2
    order = choose(j == group * (i % half_rows // 2) + 2 * (i // half_rows) + i % 2)
    for a, grad in enumerate((dq * FACTOR, dk * FACTOR, dv)):
        sorted_rows = dot(order, grad.astype(BF)).astype(BF)
        for b in range(2):
            low = HD * (3 * b + a)
            for f in range(out_ref.shape[0]):
                row = half_rows * b + 2 * f
                out_ref[f, :, low : low + HD] = sorted_rows[row : row + 2]
    i, j = iota((HD, HD), 0), iota((HD, HD), 1)
    order = choose(j == 18 * (i % 64 // 2) + 2 * (i // 64) + i % 2)
    out_t = dot_nt(order, out).astype(BF)
    for ref, half in ((keep_ref, core), (send_ref, 1 - core)):
        part = dot(out_t, dot(g, core_columns(half)).astype(BF)).astype(BF)
        for b in range(9):
            ref[:, HALF * b : HALF * (b + 1)] = part[64 * b : 64 * b + 64]


def on_device(query_s, key_s, value_s, query_t, key_t, value_t, grad_out, proj_s, proj_t):
    frames = lax.axis_size("frame")
    n_pix = lax.axis_size("pix")
    n_z = n_pix // 2
    pix = lax.axis_index("pix")
    core, z = pix % 2, pix // 2
    place = jnp.stack([core, z]).astype(jnp.int32)
    core_swap = [(p, p ^ 1) for p in range(n_pix)]
    same_core = [[2 * i + c for i in range(n_z)] for c in range(2)]

    with jax.named_scope("temporal_in"):
        flat = [a.reshape(128, a.shape[3]) for a in (query_t, key_t, value_t, grad_out)]
        sent_in = call(pack_time_kernel, 4, whole((frames, 4, 3 * HD + D), BF))(*flat)
        moved_t = lax.all_to_all(sent_in, "frame", 0, 0, tiled=True).reshape(128, 3 * HD + D)

    with jax.named_scope("spatial_grad_gather"):
        grad = grad_out[:, 0]
        own = lax.dynamic_index_in_dim(grad, core, 0, keepdims=False)
        other = lax.dynamic_index_in_dim(grad, 1 - core, 0, keepdims=False)
        other = lax.ppermute(other, "pix", core_swap)
        gathered = lax.all_gather(
            jnp.concatenate([own, other], 0), "pix", axis=0, axis_index_groups=same_core, tiled=True
        ).reshape(n_z, 2, 64, D)

    with jax.named_scope("spatial_in"):
        flat = [a.reshape(128, HD) for a in (query_s, key_s, value_s)]
        keep_s, send_s = call(
            pack_kernel, 3, (whole((n_z, 16, 4 * THREE), BF),) * 2, scalars=1
        )(place, *flat)
        packed = jnp.concatenate([keep_s, lax.ppermute(send_s, "pix", core_swap)], 1)
        moved_s = lax.all_to_all(packed, "pix", 0, 0, axis_index_groups=same_core, tiled=True)

    with jax.named_scope("temporal_attention"):
        grads_t, keep_t, send_t = call(
            temporal_kernel,
            1,
            (whole((frames, 2, GRADS), BF), whole((64, SUMS_T), BF), whole((64, SUMS_T), BF)),
            scalars=1,
            scratch=[pltpu.VMEM((HD, D), BF), pltpu.SemaphoreType.DMA],
            anywhere=1,
            mib=56,
        )(place, moved_t, proj_t)
        got_t = lax.ppermute(send_t, "pix", core_swap)

    with jax.named_scope("spatial_forward"):
        sent_out = call(
            forward_kernel,
            2,
            whole((frames, 2, GRADS + SUMS_T + SUMS_S), BF),
            scratch=[
                pltpu.VMEM((2 * frames, SUMS_S), F32),
                pltpu.VMEM(gathered.shape, BF),
                pltpu.VMEM(keep_t.shape, BF),
                pltpu.SemaphoreType.DMA((3,)),
            ],
            anywhere=3,
            mib=56,
        )(moved_s, got_t, grads_t, gathered, keep_t)

    with jax.named_scope("temporal_out"):
        home_t = lax.all_to_all(sent_out, "frame", 0, 0, tiled=True)
        back = home_t[..., :GRADS].reshape(frames, 2, 2, 3, HD).transpose(3, 2, 1, 0, 4)
        outs_t = [back[a].reshape(2, 1, 64, HD) for a in range(3)]

    with jax.named_scope("spatial_backward"):
        proj_h = lax.dynamic_slice_in_dim(proj_s, HSIZE * z, HSIZE, 0)
        proj_h = jnp.pad(proj_h, ((0, 128 - HSIZE), (0, 0)))
        own_s, other_s = call(
            backward_kernel,
            3,
            (whole((n_z, 64, THREE), BF),) * 2,
            scratch=[pltpu.VMEM((128, n_pix * 64), F32)] * 2,
        )(moved_s, gathered, proj_h)

        got_s = lax.ppermute(other_s, "pix", core_swap)

    with jax.named_scope("spatial_projection"):
        sums_s = home_t[..., GRADS + SUMS_T :].astype(F32).sum(0).reshape(2, 9, 2, HSIZE)
        sums_s = sums_s.transpose(2, 1, 0, 3).reshape(2, 18, HSIZE)
        own_sums = lax.dynamic_index_in_dim(sums_s, core, 0, keepdims=False)
        other_sums = lax.dynamic_index_in_dim(sums_s, 1 - core, 0, keepdims=False)
        sums_s = own_sums + lax.ppermute(other_sums, "pix", core_swap)
        perm = []
        for y in range(8):
            for x in range(4):
                for zz in range(n_z):
                    for c in range(2):
                        source = (y * 4 + x) * n_pix + 2 * zz + c
                        perm.append((source, (zz * 4 + x) * n_pix + 2 * y + c))
        sums_s = lax.ppermute(sums_s, ("frame", "pix"), perm)

    with jax.named_scope("spatial_out"):
        sent = call(
            ride_kernel,
            3,
            whole((n_z, 128, THREE + 36), BF),
            scratch=[pltpu.VMEM((n_z, 18, HSIZE), F32)],
        )(home_t, own_s, got_s)
        home_s = lax.all_to_all(sent, "pix", 0, 0, axis_index_groups=same_core, tiled=True)
        *outs_s, proj_t_grad, proj_s_grad = call(
            unpack_kernel,
            2,
            (whole((128, HD), BF),) * 3 + (whole((18, HSIZE), F32),) * 2,
            scalars=1,
        )(place, home_s, sums_s)
        outs_s = [a.reshape(2, 1, 64, HD) for a in outs_s]

    return (*outs_s, *outs_t, proj_s_grad, proj_t_grad)


def solution(mesh):
    rows = P(None, "frame", "pix", None)
    out_specs = (rows,) * 6 + (P("frame", "pix"),) * 2
    return jax.shard_map(
        on_device,
        mesh=mesh,
        in_specs=(rows,) * 7 + (P(), P()),
        out_specs=out_specs,
        check_vma=False,
    )
```
